512 devices in a mesh: depth: 4 (over x), row: 16 (over y, core), col: 8 (over z).
Axes of the slice: x: 4, y: 8, z: 8, core: 2. Of those that a mesh axis runs over, the one named last changes fastest.
Arguments:
- latents: bfloat16 [4, 16, 8, 3, 8, 8, 8, 256], P('depth', 'row', 'col'), may hold values from -6 to 6
- neighbours: int32 [4, 16, 8, 3, 6], P('depth', 'row', 'col'), may hold values from -1 to 1535, as said below
- owners: int32 [4, 16, 8, 3, 8], P('depth', 'row', 'col'), may hold values from -1 to 255, as said below
- conv_weight: bfloat16 [27, 256, 256], P(None, None, 'row'), may hold values from -0.078125 to 0.078125
- step_embed: float32 [256], replicated, may hold values from -6 to 6
- up_weight: bfloat16 [8, 256, 128], replicated, may hold values from -0.375 to 0.375
Outputs:
- upsampled: bfloat16 [4, 16, 8, 16, 8, 8, 8, 128], P('depth', 'row', 'col')
The draws below stay inside these ranges and needn't reach their ends.
Inputs may be any that keep to these rules, and one draw needn't show every extreme that they name: `neighbours`: entry d names the brick beside a brick's face in direction d (order -z, +z, -y, +y, -x, +x) as ((depth * 16 + row) * 8 + col) * 3 + slot; that brick lies on the same device or on the device beside it across that face. -1 where no brick is there and in every entry of an empty slot. The occupied slots of a device come first. `owners`: for an occupied slot, entry k is j * 16 + u: child k goes to slot u of the device at row j with the same depth and col; -1 in empty slots. Each device holds 1 to 3 occupied slots, and in every line of devices along row some device holds 3. Every device receives exactly 16 children, each slot once, and no device sends more than 2 children to one device.
All inputs are finite; a program needn't handle non-finite values.
Results may differ from the reference program's by a relative error of at most 0.0051.
Values may be sent and summed in bfloat16 or wider, within the bound.
No kernel may reach another device: no remote copies, remote signals or barrier semaphores. Data moves between devices by JAX's collectives and lax.ppermute only.
A program may use at most 64 MiB of HBM per device.

```python
import jax
import jax.numpy as jnp
from jax import lax

C = 256
CO = 128
E = 8
CAP = 3
BX = 2
OCAP = 16
N_DEPTH = 4
N_ROW = 16
N_COL = 8


def scene_layout(key):
    device_count = N_DEPTH * N_ROW * N_COL
    places = 2 * BX
    half_rows = N_ROW // 2
    groups = N_DEPTH * N_COL
    key_pairs, key_force, key_side, key_rank, key_turn = jax.random.split(jax.random.fold_in(key, 17), 5)
    firsts = jax.random.randint(key_pairs, (groups, half_rows), 1, CAP + 1)
    forced_pair = jax.random.randint(key_force, (groups, 1), 0, half_rows)
    forced_side = jax.random.randint(key_side, (groups, 1), 0, 2)
    firsts = jnp.where(jnp.arange(half_rows)[None, :] == forced_pair, 1 + forced_side * (CAP - 1), firsts)
    pair_counts = jnp.stack([firsts, CAP + 1 - firsts], axis=2).reshape(N_DEPTH, N_COL, N_ROW)
    counts = pair_counts.transpose(0, 2, 1).astype(jnp.int32)
    ranking = jax.vmap(lambda subkey: jax.random.permutation(subkey, places))(jax.random.split(key_rank, N_ROW * N_COL))
    ranking = ranking.reshape(N_ROW, N_COL, places).astype(jnp.int32)
    filled = ranking[None] < counts[..., None]
    slot_at = jnp.where(filled, ranking[None], -1)
    device_ids = jnp.arange(device_count, dtype=jnp.int32).reshape(N_DEPTH, N_ROW, N_COL)
    global_ids = jnp.where(filled, device_ids[..., None] * CAP + slot_at, -1)
    brick_grid = global_ids.reshape(N_DEPTH, N_ROW, N_COL, 2, BX).transpose(0, 1, 3, 2, 4).reshape(N_DEPTH, N_ROW * 2, N_COL * BX)
    grid_padded = jnp.pad(brick_grid, 1, constant_values=-1)
    place_ids = jnp.arange(places, dtype=jnp.int32)
    full_shape = (N_DEPTH, N_ROW, N_COL, places)
    coord_z = jnp.broadcast_to(jnp.arange(N_DEPTH, dtype=jnp.int32)[:, None, None, None] + 1, full_shape)
    coord_y = jnp.broadcast_to(jnp.arange(N_ROW, dtype=jnp.int32)[None, :, None, None] * 2 + (place_ids // BX)[None, None, None, :] + 1, full_shape)
    coord_x = jnp.broadcast_to(jnp.arange(N_COL, dtype=jnp.int32)[None, None, :, None] * BX + (place_ids % BX)[None, None, None, :] + 1, full_shape)
    steps_list = [(-1, 0, 0), (1, 0, 0), (0, -1, 0), (0, 1, 0), (0, 0, -1), (0, 0, 1)]
    adjacent = jnp.stack([grid_padded[coord_z + step_z, coord_y + step_y, coord_x + step_x] for step_z, step_y, step_x in steps_list], axis=-1)
    matches = (slot_at[..., None] == jnp.arange(CAP, dtype=jnp.int32)).astype(jnp.int32)
    near_ids = jnp.sum(matches[..., None] * (adjacent[..., None, :] + 1), axis=3) - 1
    children_count = 8 * counts
    first_serial = jnp.cumsum(children_count, axis=1) - children_count
    child_ids = jnp.arange(CAP * 8, dtype=jnp.int32)
    serial = first_serial[..., None] + child_ids
    is_live = child_ids < children_count[..., None]
    rotation = jax.random.randint(key_turn, (N_DEPTH, 1, N_COL, 1), 0, N_ROW * OCAP)
    shifted = (serial + rotation) % (N_ROW * OCAP)
    owner_ids = jnp.where(is_live, shifted % N_ROW * OCAP + shifted // N_ROW, -1)
    return (near_ids.reshape(N_DEPTH, N_ROW, N_COL, CAP, 6).astype(jnp.int32), owner_ids.reshape(N_DEPTH, N_ROW, N_COL, CAP, 8).astype(jnp.int32))


def draw_neighbours(key, part):
    return scene_layout(key)[0]


def draw_owners(key, part):
    return scene_layout(key)[1]


def block_levels(own_key, dims, cuts, low, high):
    def one(axis_at, blocks):
        steps = jax.random.uniform(jax.random.fold_in(jax.random.fold_in(own_key, 6), axis_at), (blocks,), jnp.float32, low / len(cuts), high / len(cuts))
        return jnp.repeat(jnp.exp(steps), dims[axis_at] // blocks).reshape((-1,) + (1,) * (len(dims) - axis_at - 1))

    gain = one(*cuts[0])
    for cut in cuts[1:]:
        gain = gain * one(*cut)
    return gain


def bell_draw(own_key, dims, scale, most, cuts=(), held_as=jnp.bfloat16):
    level = block_levels(own_key, dims, cuts, -0.22, 0.18) if cuts else 1.0
    entries = jax.random.normal(own_key, dims, jnp.float32) * scale * level
    return jnp.minimum(jnp.maximum(entries, -most), most).astype(held_as)


def setup_inputs(seed: int = 0) -> dict:
    keys = jax.random.split(jax.random.key(seed), 7)
    latents = bell_draw(keys[0], (N_DEPTH, N_ROW, N_COL, CAP, E, E, E, C), 1.0, 6.0, ((0, 4), (1, 16), (2, 8)))
    neighbours = draw_neighbours(jax.random.fold_in(keys[6], 71), 0)
    owners = draw_owners(jax.random.fold_in(keys[6], 71), 0)
    conv_weight = bell_draw(keys[3], (27, C, C), (27 * C) ** -0.5, 0.078125, ((2, 16),))
    step_embed = bell_draw(keys[4], (C,), 1.0, 6.0, (), jnp.float32)
    up_weight = bell_draw(keys[5], (8, C, CO), C ** -0.5, 0.375)
    return dict(latents=latents, neighbours=neighbours, owners=owners, conv_weight=conv_weight, step_embed=step_embed, up_weight=up_weight)


def normed_silu(values):
    mean_square = lax.optimization_barrier(jnp.mean(values * values, axis=-1, keepdims=True))
    return jax.nn.silu(values * lax.rsqrt(mean_square + 1e-06))

def face_of(first_input, near_ids, direction):
    face_layer = E - 1 if direction % 2 == 0 else 0
    if direction < 2:
        face_table = first_input[:, face_layer]
    elif direction < 4:
        face_table = first_input[:, :, face_layer]
    else:
        face_table = first_input[:, :, :, face_layer]
    near_index = near_ids[:, direction]
    fetched = face_table[jnp.maximum(near_index, 0)]
    return jnp.where((near_index >= 0)[:, None, None, None], fetched, jnp.zeros_like(fetched))

def reference(latents, neighbours, owners, conv_weight, step_embed, up_weight):
    device_count = N_DEPTH * N_ROW * N_COL
    bricks = device_count * CAP
    half_len = E // 2
    latent_bricks = latents.reshape(bricks, E, E, E, C)
    near_ids = neighbours.reshape(bricks, 6)
    first_input = normed_silu(latent_bricks.astype(jnp.float32)).astype(jnp.bfloat16)
    face_list = [face_of(first_input, near_ids, direction) for direction in range(6)]
    matrix = conv_weight.reshape(27 * C, C)

    def per_device(pieces):
        latent_block, first_block, below_z, above_z, below_y, above_y, below_x, above_x = pieces
        padded = jnp.zeros((CAP, E + 2, E + 2, E + 2, C), first_block.dtype)
        padded = padded.at[:, 1:-1, 1:-1, 1:-1].set(first_block)
        padded = padded.at[:, 0, 1:-1, 1:-1].set(below_z)
        padded = padded.at[:, E + 1, 1:-1, 1:-1].set(above_z)
        padded = padded.at[:, 1:-1, 0, 1:-1].set(below_y)
        padded = padded.at[:, 1:-1, E + 1, 1:-1].set(above_y)
        padded = padded.at[:, 1:-1, 1:-1, 0].set(below_x)
        padded = padded.at[:, 1:-1, 1:-1, E + 1].set(above_x)
        columns = jnp.concatenate([padded[:, shift_z:shift_z + E, shift_y:shift_y + E, shift_x:shift_x + E] for shift_z in range(3) for shift_y in range(3) for shift_x in range(3)], axis=-1)
        columns = columns.reshape(CAP * E * E * E, 27 * C)
        conv_sum = jnp.dot(columns, matrix, preferred_element_type=jnp.float32).reshape(CAP, E, E, E, C) + step_embed
        refined = (latent_block.astype(jnp.float32) + conv_sum).astype(jnp.bfloat16)
        octants = refined.reshape(CAP, 2, half_len, 2, half_len, 2, half_len, C).transpose(0, 1, 3, 5, 2, 4, 6, 7)
        return octants.reshape(CAP * 8, half_len ** 3, C)
    stacked = tuple((member.reshape((device_count, CAP) + member.shape[1:]) for member in [latent_bricks, first_input] + face_list))
    octants = lax.map(per_device, stacked).reshape(bricks * 8, half_len ** 3, C)
    targets = owners.reshape(N_DEPTH, N_ROW, N_COL, CAP * 8)
    depth_ids = jnp.arange(N_DEPTH, dtype=jnp.int32)[:, None, None, None]
    col_ids = jnp.arange(N_COL, dtype=jnp.int32)[None, None, :, None]
    flat_slot = ((depth_ids * N_ROW + targets // OCAP) * N_COL + col_ids) * OCAP + targets % OCAP
    placed = jnp.where(targets >= 0, flat_slot, device_count * OCAP).astype(jnp.int32)
    sources = jnp.zeros((device_count * OCAP,), jnp.int32).at[placed.reshape(-1)].set(jnp.arange(bricks * 8, dtype=jnp.int32), mode='drop')
    expand = up_weight.transpose(1, 0, 2).reshape(C, 8 * CO)

    def grow_device(source_ids):
        gathered = octants[source_ids].reshape(OCAP * half_len ** 3, C)
        spread = jnp.dot(gathered, expand, preferred_element_type=jnp.float32)
        spread = spread.reshape(OCAP, half_len, half_len, half_len, 2, 2, 2, CO).transpose(0, 1, 4, 2, 5, 3, 6, 7)
        return spread.reshape(OCAP, E, E, E, CO).astype(jnp.bfloat16)
    upsampled = lax.map(grow_device, sources.reshape(device_count, OCAP))
    return upsampled.reshape(N_DEPTH, N_ROW, N_COL, OCAP, E, E, E, CO)
```

```python
import jax
import jax.numpy as jnp
from jax import lax
from jax.experimental import pallas as pl
from jax.experimental.pallas import tpu as pltpu
from jax.sharding import PartitionSpec as P

OCAP = 16
VMEM = pltpu.VMEM
SMEM = pltpu.SMEM
MB = 1024 * 1024


def whole(count):
    return [pl.BlockSpec(memory_space=VMEM)] * count


def norm_kernel(lat_ref, fi_ref, zlo_ref, zhi_ref, ylo_ref, yhi_ref, xlo_ref, xhi_ref, rows_ref):
    slots, edge, plane, _ = lat_ref.shape
    lanes = rows_ref.shape[-1]
    pieces = rows_ref.shape[0]
    for b in range(slots):
        for z in range(edge):
            v = lat_ref[b, z].astype(jnp.float32)
            mean_square = jnp.mean(v * v, axis=-1, keepdims=True)
            n = v * lax.rsqrt(mean_square + 1e-06)
            s = n / (1.0 + jnp.exp(-n))
            half = s.astype(jnp.bfloat16)
            fi_ref[b, z] = half
            if z == 0:
                zlo_ref[b] = half
            if z == edge - 1:
                zhi_ref[b] = half
            for p in range(pieces):
                rows_ref[p, pl.ds(z * plane, plane), :] = s[:, p * lanes : (p + 1) * lanes]
        for p in range(pieces):
            cols = pl.ds(p * lanes, lanes)
            xlo_ref[b, :, cols] = rows_ref[p, pl.ds(0, plane, stride=edge), :].astype(jnp.bfloat16)
            xhi_ref[b, :, cols] = rows_ref[p, pl.ds(edge - 1, plane, stride=edge), :].astype(
                jnp.bfloat16
            )
            low = [rows_ref[p, pl.ds(z * plane, edge), :] for z in range(edge)]
            ylo_ref[b, :, cols] = jnp.concatenate(low, axis=0).astype(jnp.bfloat16)
            high = [rows_ref[p, pl.ds(z * plane + plane - edge, edge), :] for z in range(edge)]
            yhi_ref[b, :, cols] = jnp.concatenate(high, axis=0).astype(jnp.bfloat16)


def columns_kernel(
    pick_ref, fi_ref, zlo, zhi, ylo, yhi, xlo, xhi, rz0, rz1, ry0, ry1, rx0, rx1, out_ref, table_ref, ybuf_ref, xbuf_ref
):
    slots, edge, plane, chan = fi_ref.shape
    near = (zhi, zlo, yhi, ylo, xhi, xlo)
    far = (rz0, rz1, ry0, ry1, rx0, rx1)
    for d in range(6):
        table_ref[d, 0:slots] = near[d][...]
        table_ref[d, slots : 2 * slots] = far[d][...]
        table_ref[d, 2 * slots] = jnp.zeros((plane, chan), jnp.bfloat16)
    at_x = lax.rem(lax.broadcasted_iota(jnp.int32, (plane + 2 * edge, chan), 0), edge)

    def put(b, z, rows, left, right):
        zero = jnp.zeros((edge, chan), jnp.float32)

        def spread(halo):
            mid = jnp.broadcast_to(halo[:, None, :], (edge, edge, chan)).reshape(plane, chan)
            return jnp.concatenate([zero, mid, zero], axis=0)

        count = plane + 2 * edge
        moved = (
            jnp.where(at_x == 0, spread(left), pltpu.roll(rows, 1, 0)),
            rows,
            jnp.where(at_x == edge - 1, spread(right), pltpu.roll(rows, count - 1, 0)),
        )
        for dx in range(3):
            for dy in range(3):
                tap = dy * 3 + dx
                out_ref[b, z, :, tap * chan : (tap + 1) * chan] = moved[dx][
                    dy * edge : dy * edge + plane
                ].astype(jnp.bfloat16)

    def brick(b, _):
        zero = jnp.zeros((edge, chan), jnp.float32)
        for side in range(2):
            cap = table_ref[side, pick_ref[b * 6 + side]].astype(jnp.float32)
            rows = jnp.concatenate([zero, cap, zero], axis=0)
            put(b, side * (edge + 1), rows, zero, zero)
            ybuf_ref[side] = table_ref[2 + side, pick_ref[b * 6 + 2 + side]].astype(jnp.float32)
            xbuf_ref[side] = table_ref[4 + side, pick_ref[b * 6 + 4 + side]].astype(jnp.float32)

        def layer(z, _):
            strip = pl.ds(pl.multiple_of(z * edge, edge), edge)
            rows = jnp.concatenate(
                [ybuf_ref[0, strip, :], fi_ref[b, z].astype(jnp.float32), ybuf_ref[1, strip, :]], axis=0
            )
            put(b, z + 1, rows, xbuf_ref[0, strip, :], xbuf_ref[1, strip, :])
            return 0

        lax.fori_loop(0, edge, layer, 0)
        return 0

    lax.fori_loop(0, slots, brick, 0)


def conv_kernel(place_ref, cols_ref, w_ref, lat_ref, emb_ref, out_ref, acc_ref):
    step = pl.program_id(0)
    slots, edge, plane, chan = lat_ref.shape
    half = edge // 2
    for b in range(slots):
        lhs = cols_ref[b, pl.ds(step, edge)].reshape(edge * plane, cols_ref.shape[-1])
        part = lax.dot_general(
            lhs, w_ref[...], (((1,), (1,)), ((), ())), preferred_element_type=jnp.float32
        )

        @pl.when(step == 0)
        def _():
            acc_ref[b] = part

        @pl.when(step > 0)
        def _():
            acc_ref[b] += part

    @pl.when(step == pl.num_programs(0) - 1)
    def _():
        in_low = lax.broadcasted_iota(jnp.int32, (edge * half // 2, edge, chan), 1) < half
        for b in range(slots):
            for kz in range(2):
                base = kz * half
                lat = lat_ref[b, base : base + half].astype(jnp.float32).reshape(half * plane, chan)
                total = acc_ref[b, base * plane : (base + half) * plane]
                refined = lat + (total + emb_ref[...])
                pairs = refined.reshape(half, 2, half // 2, 2, edge, chan)
                for ky in range(2):
                    first = pairs[:, ky, :, 0].reshape(-1, edge, chan)
                    second = pairs[:, ky, :, 1].reshape(-1, edge, chan)
                    low_mask = in_low[: first.shape[0]]
                    turned = (
                        pltpu.roll(first, half, 1),
                        pltpu.roll(second, half, 1),
                    )
                    child = (
                        jnp.where(low_mask, first, turned[1]),
                        jnp.where(low_mask, turned[0], second),
                    )
                    for kx in range(2):
                        k = b * 8 + kz * 4 + ky * 2 + kx
                        value = child[kx].reshape(half**3, chan).astype(jnp.bfloat16)

                        @pl.when(place_ref[k] >= 0)
                        def _():
                            out_ref[place_ref[k]] = value


def grow_kernel(source_ref, child_ref, up_ref, out_ref, rows_ref):
    step = pl.program_id(0)
    each = out_ref.shape[0]
    co = up_ref.shape[-1]
    voxels = child_ref.shape[1]
    lhs = jnp.concatenate([child_ref[source_ref[step * each + j]] for j in range(each)], axis=0)
    for pz in range(2):
        for py in range(2):
            p = pz * 4 + py * 2
            mats = jnp.concatenate([up_ref[p], up_ref[p + 1]], axis=1)
            res = jnp.dot(lhs, mats, preferred_element_type=jnp.float32)
            rows_ref[pl.ds(0, each * voxels, stride=2), :] = res[:, :co]
            rows_ref[pl.ds(1, each * voxels, stride=2), :] = res[:, co:]
            out_ref[:, :, pz, :, py] = (
                rows_ref[...].reshape(each, 4, 4, 8, co).astype(jnp.bfloat16)
            )


def body(latents, neighbours, owners, conv_weight, step_embed, up_weight):
    rows_n = lax.axis_size("row")
    cols_n = lax.axis_size("col")
    own_row = lax.axis_index("row")
    own_index = (lax.axis_index("depth") * rows_n + own_row) * cols_n + lax.axis_index("col")
    slots, edge, chan = latents.shape[3], latents.shape[4], latents.shape[-1]
    plane = edge * edge
    taps = conv_weight.shape[0]
    own_out = conv_weight.shape[2]
    co = up_weight.shape[-1]
    owner_ids = owners.reshape(slots * 8)

    note = jnp.zeros((own_out, 128), jnp.bfloat16)
    note = note.at[0, : slots * 8].set(owner_ids.astype(jnp.bfloat16))
    piece = conv_weight.transpose(2, 0, 1).reshape(own_out, taps * chan)
    weight = lax.all_gather(jnp.concatenate([piece, note], axis=1), "row", axis=0, tiled=True)

    lat = latents.reshape(slots, edge, plane, chan)
    face = jax.ShapeDtypeStruct((slots, plane, chan), jnp.bfloat16)
    fi, zlo, zhi, ylo, yhi, xlo, xhi = pl.pallas_call(
        norm_kernel,
        out_shape=[jax.ShapeDtypeStruct(lat.shape, jnp.bfloat16)] + [face] * 6,
        in_specs=whole(1),
        out_specs=whole(7),
        scratch_shapes=[pltpu.VMEM((chan // 128, edge * plane, 128), jnp.float32)],
        compiler_params=pltpu.CompilerParams(vmem_limit_bytes=32 * MB),
        cost_estimate=pl.CostEstimate(flops=4 * MB, bytes_accessed=2 * MB, transcendentals=MB),
    )(lat)

    def shift(face, axis, step):
        count = lax.axis_size(axis)
        pairs = [(i, i + step) for i in range(count) if 0 <= i + step < count]
        return lax.ppermute(face, axis, pairs)

    far = (
        shift(zhi, "depth", 1),
        shift(zlo, "depth", -1),
        shift(yhi, "row", 1),
        shift(ylo, "row", -1),
        shift(xhi, "col", 1),
        shift(xlo, "col", -1),
    )
    near_ids = neighbours.reshape(slots, 6)
    strides = jnp.array([-rows_n * cols_n, rows_n * cols_n, -cols_n, cols_n, -1, 1], jnp.int32)
    near_dev = near_ids // slots
    near_slot = near_ids % slots
    pick = jnp.where(
        near_ids < 0,
        2 * slots,
        jnp.where(
            near_dev == own_index,
            near_slot,
            jnp.where(near_dev == own_index + strides[None, :], slots + near_slot, 2 * slots),
        ),
    ).reshape(-1)

    columns = pl.pallas_call(
        columns_kernel,
        out_shape=jax.ShapeDtypeStruct((slots, edge + 2, plane, 9 * chan), jnp.bfloat16),
        in_specs=[pl.BlockSpec(memory_space=SMEM)] + whole(13),
        out_specs=pl.BlockSpec(memory_space=VMEM),
        scratch_shapes=[
            pltpu.VMEM((6, 2 * slots + 1, plane, chan), jnp.bfloat16),
            pltpu.VMEM((2, plane, chan), jnp.float32),
            pltpu.VMEM((2, plane, chan), jnp.float32),
        ],
        compiler_params=pltpu.CompilerParams(vmem_limit_bytes=40 * MB),
        cost_estimate=pl.CostEstimate(flops=16 * MB, bytes_accessed=12 * MB, transcendentals=0),
    )(pick, fi, zlo, zhi, ylo, yhi, xlo, xhi, *far)

    send_cap = 2
    is_valid = owner_ids >= 0
    target_row = jnp.where(is_valid, owner_ids // OCAP, -1)
    serial = jnp.arange(slots * 8, dtype=jnp.int32)
    before = serial[None, :] < serial[:, None]
    rank = jnp.sum(((target_row[None, :] == target_row[:, None]) & before).astype(jnp.int32), axis=1)
    place = jnp.where(is_valid, target_row * send_cap + rank, -1)

    outgoing = pl.pallas_call(
        conv_kernel,
        grid=(3,),
        out_shape=jax.ShapeDtypeStruct((rows_n * send_cap, plane, chan), jnp.bfloat16),
        in_specs=[
            pl.BlockSpec(memory_space=SMEM),
            pl.BlockSpec(memory_space=VMEM),
            pl.BlockSpec((chan, 9 * chan), lambda i: (0, i)),
            pl.BlockSpec(memory_space=VMEM),
            pl.BlockSpec(memory_space=VMEM),
        ],
        out_specs=pl.BlockSpec(memory_space=VMEM),
        scratch_shapes=[pltpu.VMEM((slots, edge * plane, chan), jnp.float32)],
        compiler_params=pltpu.CompilerParams(vmem_limit_bytes=48 * MB),
        cost_estimate=pl.CostEstimate(flops=5400 * MB, bytes_accessed=14 * MB, transcendentals=0),
    )(place, columns, weight, lat, step_embed.reshape(1, chan))

    arrived = lax.all_to_all(
        outgoing.reshape(rows_n, send_cap * plane, chan), "row", split_axis=0, concat_axis=0, tiled=True
    ).reshape(rows_n * send_cap, plane, chan)

    notes = weight[::own_out, taps * chan : taps * chan + slots * 8].astype(jnp.int32)
    mine = (notes >= 0) & (notes // OCAP == own_row)
    again = jnp.any(mine[:, None, :] & before[None], axis=2)
    origin = jnp.arange(rows_n, dtype=jnp.int32)[:, None] * send_cap + again.astype(jnp.int32)
    wanted = jnp.arange(OCAP, dtype=jnp.int32)[:, None, None]
    source = jnp.sum(jnp.where(mine[None] & (notes[None] % OCAP == wanted), origin[None], 0), axis=(1, 2))

    half = edge // 2
    each = 4
    grown = pl.pallas_call(
        grow_kernel,
        grid_spec=pltpu.PrefetchScalarGridSpec(
            num_scalar_prefetch=1,
            grid=(OCAP // each,),
            in_specs=whole(2),
            out_specs=pl.BlockSpec((each, half, 2, half, 2, edge, co), lambda i, s: (i, 0, 0, 0, 0, 0, 0)),
            scratch_shapes=[pltpu.VMEM((each * plane * 2, co), jnp.float32)],
        ),
        out_shape=jax.ShapeDtypeStruct((OCAP, half, 2, half, 2, edge, co), jnp.bfloat16),
        compiler_params=pltpu.CompilerParams(vmem_limit_bytes=32 * MB),
        cost_estimate=pl.CostEstimate(flops=540 * MB, bytes_accessed=4 * MB, transcendentals=0),
    )(source, arrived, up_weight)
    return grown.reshape(1, 1, 1, OCAP, edge, edge, edge, co)


def solution(mesh):
    return jax.shard_map(
        body,
        mesh=mesh,
        in_specs=(
            P("depth", "row", "col", None, None, None, None, None),
            P("depth", "row", "col", None, None),
            P("depth", "row", "col", None, None),
            P(None, None, "row"),
            P(),
            P(),
        ),
        out_specs=P("depth", "row", "col", None, None, None, None, None),
        check_vma=False,
    )
```

```python
import jax
import jax.numpy as jnp
from jax import lax
from jax.experimental import pallas as pl
from jax.experimental.pallas import tpu as pltpu
from jax.sharding import PartitionSpec as P

OCAP = 16
VMEM = pltpu.VMEM
SMEM = pltpu.SMEM
MB = 1024 * 1024


def whole(count):
    return [pl.BlockSpec(memory_space=VMEM)] * count


def norm_kernel(lat_ref, fi_ref, zlo_ref, zhi_ref, ylo_ref, yhi_ref, xlo_ref, xhi_ref, rows_ref):
    slots, edge, plane, _ = lat_ref.shape
    lanes = rows_ref.shape[-1]
    pieces = rows_ref.shape[0]
    for b in range(slots):
        for z in range(edge):
            v = lat_ref[b, z].astype(jnp.float32)
            mean_square = jnp.mean(v * v, axis=-1, keepdims=True)
            n = v * lax.rsqrt(mean_square + 1e-06)
            s = n / (1.0 + jnp.exp(-n))
            half = s.astype(jnp.bfloat16)
            fi_ref[b, z] = half
            if z == 0:
                zlo_ref[b] = half
            if z == edge - 1:
                zhi_ref[b] = half
            for p in range(pieces):
                rows_ref[p, pl.ds(z * plane, plane), :] = s[:, p * lanes : (p + 1) * lanes]
        for p in range(pieces):
            cols = pl.ds(p * lanes, lanes)
            xlo_ref[b, :, cols] = rows_ref[p, pl.ds(0, plane, stride=edge), :].astype(jnp.bfloat16)
            xhi_ref[b, :, cols] = rows_ref[p, pl.ds(edge - 1, plane, stride=edge), :].astype(
                jnp.bfloat16
            )
            low = [rows_ref[p, pl.ds(z * plane, edge), :] for z in range(edge)]
            ylo_ref[b, :, cols] = jnp.concatenate(low, axis=0).astype(jnp.bfloat16)
            high = [rows_ref[p, pl.ds(z * plane + plane - edge, edge), :] for z in range(edge)]
            yhi_ref[b, :, cols] = jnp.concatenate(high, axis=0).astype(jnp.bfloat16)


def quarter_kernel(owners_ref, weight_ref, out_ref):
    taps, rows, chan = weight_ref.shape
    count = out_ref.shape[1] // chan
    wide = out_ref.shape[1] - count * chan
    first = colour_here() * count
    lane = lax.broadcasted_iota(jnp.int32, (rows, wide), 1)
    note = jnp.zeros((rows, wide), jnp.int32)
    children = owners_ref.shape[-1]
    for i in range(owners_ref.shape[-2] * children):
        note = jnp.where(lane == i, owners_ref[0, 0, 0, i // children, i % children], note)
    for j in range(count):
        out_ref[:, j * chan : (j + 1) * chan] = weight_ref[jnp.minimum(first + j, taps - 1)]
    out_ref[:, count * chan :] = note.astype(jnp.float32).astype(jnp.bfloat16)


def columns_kernel(
    near_ref, fi_ref, zlo, zhi, ylo, yhi, xlo, xhi, rz0, rz1, ry0, ry1, rx0, rx1, out_ref, table_ref, ybuf_ref, xbuf_ref
):
    slots, edge, plane, chan = fi_ref.shape
    near = (zhi, zlo, yhi, ylo, xhi, xlo)
    far = (rz0, rz1, ry0, ry1, rx0, rx1)
    for d in range(6):
        table_ref[d, 0:slots] = near[d][...]
        table_ref[d, slots : 2 * slots] = far[d][...]
        table_ref[d, 2 * slots] = jnp.zeros((plane, chan), jnp.bfloat16)
    out_ref[9] = jnp.zeros(out_ref.shape[1:], jnp.bfloat16)
    at_x = lax.rem(lax.broadcasted_iota(jnp.int32, (plane + 2 * edge, chan), 0), edge)
    rows_n = lax.axis_size("row")
    cols_n = lax.axis_size("col")
    own = (lax.axis_index("depth") * rows_n + lax.axis_index("row")) * cols_n + lax.axis_index("col")
    steps = (-rows_n * cols_n, rows_n * cols_n, -cols_n, cols_n, -1, 1)

    def chosen(b, d):
        named = near_ref[0, 0, 0, b, d]
        here = named - own * slots
        there = named - (own + steps[d]) * slots
        is_here = (named >= 0) & (here >= 0) & (here < slots)
        is_there = (named >= 0) & (there >= 0) & (there < slots)
        index = jnp.where(is_here, here, jnp.where(is_there, slots + there, 2 * slots))
        return table_ref[d, index].astype(jnp.float32)

    def put(b, z, rows, left, right):
        zero = jnp.zeros((edge, chan), jnp.float32)

        def spread(halo):
            mid = jnp.broadcast_to(halo[:, None, :], (edge, edge, chan)).reshape(plane, chan)
            return jnp.concatenate([zero, mid, zero], axis=0)

        count = plane + 2 * edge
        moved = (
            jnp.where(at_x == 0, spread(left), pltpu.roll(rows, 1, 0)),
            rows,
            jnp.where(at_x == edge - 1, spread(right), pltpu.roll(rows, count - 1, 0)),
        )
        for dx in range(3):
            for dy in range(3):
                out_ref[dy * 3 + dx, b, z] = moved[dx][dy * edge : dy * edge + plane].astype(
                    jnp.bfloat16
                )

    def brick(b, _):
        zero = jnp.zeros((edge, chan), jnp.float32)
        for side in range(2):
            rows = jnp.concatenate([zero, chosen(b, side), zero], axis=0)
            put(b, side * (edge + 1), rows, zero, zero)
            ybuf_ref[side] = chosen(b, 2 + side)
            xbuf_ref[side] = chosen(b, 4 + side)

        def layer(z, _):
            strip = pl.ds(pl.multiple_of(z * edge, edge), edge)
            rows = jnp.concatenate(
                [ybuf_ref[0, strip, :], fi_ref[b, z].astype(jnp.float32), ybuf_ref[1, strip, :]], axis=0
            )
            put(b, z + 1, rows, xbuf_ref[0, strip, :], xbuf_ref[1, strip, :])
            return 0

        lax.fori_loop(0, edge, layer, 0)
        return 0

    lax.fori_loop(0, slots, brick, 0)


def colour_here():
    return lax.rem(lax.axis_index("depth") + 2 * lax.axis_index("col"), 4)


def core_here():
    return lax.rem(lax.axis_index("row"), 2)


def tap_rows(cols_ref, b, first, count):
    edge, plane, chan = cols_ref.shape[2] - 2, cols_ref.shape[3], cols_ref.shape[4]
    out = []
    for j in range(count):
        tap = first + j
        live = tap < 27
        which = jnp.where(live, lax.rem(tap, 9), 9)
        layer = jnp.where(live, lax.div(tap, 9), 0)
        out.append(cols_ref[which, b, pl.ds(layer, edge)].reshape(edge * plane, chan))
    return out


def times(lhs, weight):
    return lax.dot_general(
        jnp.concatenate(lhs, axis=1), weight, (((1,), (1,)), ((), ())), preferred_element_type=jnp.float32
    )


def own_kernel(cols_ref, own_ref, acc_ref):
    chan = cols_ref.shape[4]
    count = own_ref.shape[1] // chan
    first = colour_here() * count
    for b in range(acc_ref.shape[0]):
        acc_ref[b] = times(tap_rows(cols_ref, b, first, count), own_ref[:, : count * chan])


def side_kernel(cols_ref, xw_ref, zw_ref, old_ref, acc_ref):
    chan = cols_ref.shape[4]
    count, part = xw_ref.shape[1] // chan, zw_ref.shape[1] // chan
    core, colour = core_here(), colour_here()
    x_first = lax.rem(colour + 3 + 2 * core, 4) * count
    z_first = lax.rem(colour + 2, 4) * count + core * (count - part)
    for b in range(acc_ref.shape[0]):
        got = times(tap_rows(cols_ref, b, x_first, count), xw_ref[:, : count * chan])
        got += times(tap_rows(cols_ref, b, z_first, part), zw_ref[...])
        acc_ref[b] = old_ref[b] + got


def last_kernel(owners_ref, cols_ref, xw_ref, zw_ref, lat_ref, emb_ref, old_ref, out_ref):
    slots, edge, plane, chan = lat_ref.shape
    half = edge // 2
    count, part = xw_ref.shape[1] // chan, zw_ref.shape[1] // chan
    rest = count - part
    core, colour = core_here(), colour_here()
    x_first = lax.rem(colour + 1 + 2 * core, 4) * count
    z_first = lax.rem(colour + 2, 4) * count + (1 - core) * part
    lanes = pl.ds(pl.multiple_of((1 - core) * (part - rest) * chan, chan), rest * chan)

    targets = [owners_ref[0, 0, 0, i // 8, i % 8] for i in range(slots * 8)]
    target_rows = [lax.shift_right_arithmetic(t, 4) for t in targets]
    in_low = lax.broadcasted_iota(jnp.int32, (half * half // 2, edge, chan), 1) < half
    for b in range(slots):
        got = times(tap_rows(cols_ref, b, x_first, count), xw_ref[:, : count * chan])
        got += times(tap_rows(cols_ref, b, z_first, rest), zw_ref[:, lanes])
        total = old_ref[b] + got
        lat = lat_ref[b].astype(jnp.float32).reshape(edge * plane, chan)
        refined = lat + (total + emb_ref[...])
        pairs = refined.reshape(2, half, 2, half // 2, 2, edge, chan)
        for kz in range(2):
            for ky in range(2):
                first = pairs[kz, :, ky, :, 0].reshape(-1, edge, chan)
                second = pairs[kz, :, ky, :, 1].reshape(-1, edge, chan)
                child = (
                    jnp.where(in_low, first, pltpu.roll(second, half, 1)),
                    jnp.where(in_low, pltpu.roll(first, half, 1), second),
                )
                for kx in range(2):
                    k = b * 8 + kz * 4 + ky * 2 + kx
                    value = child[kx].reshape(half**3, chan).astype(jnp.bfloat16)
                    rank = 0
                    for j in range(k):
                        rank += (target_rows[j] == target_rows[k]).astype(jnp.int32)
                    place = target_rows[k] * 2 + rank

                    @pl.when(targets[k] >= 0)
                    def _():
                        out_ref[place] = value


def grow_kernel(source_ref, child_ref, up_ref, out_ref, rows_ref):
    step = pl.program_id(0)
    each = out_ref.shape[0]
    co = up_ref.shape[-1]
    voxels = child_ref.shape[1]
    lhs = jnp.concatenate([child_ref[source_ref[step * each + j]] for j in range(each)], axis=0)
    for pz in range(2):
        for py in range(2):
            p = pz * 4 + py * 2
            mats = jnp.concatenate([up_ref[p], up_ref[p + 1]], axis=1)
            res = jnp.dot(lhs, mats, preferred_element_type=jnp.float32)
            rows_ref[pl.ds(0, each * voxels, stride=2), :] = res[:, :co]
            rows_ref[pl.ds(1, each * voxels, stride=2), :] = res[:, co:]
            out_ref[:, :, pz, :, py] = (
                rows_ref[...].reshape(each, 4, 4, 8, co).astype(jnp.bfloat16)
            )


def body(latents, neighbours, owners, conv_weight, step_embed, up_weight):
    rows_n = lax.axis_size("row")
    cols_n = lax.axis_size("col")
    slots, edge, chan = latents.shape[3], latents.shape[4], latents.shape[-1]
    plane = edge * edge
    taps = conv_weight.shape[0]
    own_out = conv_weight.shape[2]
    co = up_weight.shape[-1]
    quarter = (taps + 1) // 4
    part = quarter // 2 + 1
    core = core_here()

    smem = pl.BlockSpec(memory_space=SMEM)
    piece = pl.pallas_call(
        quarter_kernel,
        out_shape=jax.ShapeDtypeStruct((own_out, quarter * chan + 128), jnp.bfloat16),
        in_specs=[smem] + whole(1),
        out_specs=pl.BlockSpec(memory_space=VMEM),
        compiler_params=pltpu.CompilerParams(vmem_limit_bytes=4 * MB),
    )(owners, conv_weight.transpose(0, 2, 1))
    own_w = lax.all_gather(piece, "row", axis=0, tiled=True)
    depth_n = lax.axis_size("depth")
    x_pairs = [
        (d * rows_n + r, (d + 1 - 2 * (r % 2)) % depth_n * rows_n + r)
        for d in range(depth_n)
        for r in range(rows_n)
    ]
    z_pairs = [
        (r * cols_n + c, r * cols_n + (c + 1 - 2 * (r % 2)) % cols_n)
        for r in range(rows_n)
        for c in range(cols_n)
    ]
    swap = [(r, r ^ 1) for r in range(rows_n)]
    z_send = lax.dynamic_slice(own_w, (0, core * (quarter - part) * chan), (chan, part * chan))
    x_got = lax.ppermute(own_w, ("depth", "row"), x_pairs)
    z_got = lax.ppermute(z_send, ("row", "col"), z_pairs)
    lat, own_w = lax.optimization_barrier((latents.reshape(slots, edge, plane, chan), own_w))
    face = jax.ShapeDtypeStruct((slots, plane, chan), jnp.bfloat16)
    fi, zlo, zhi, ylo, yhi, xlo, xhi = pl.pallas_call(
        norm_kernel,
        out_shape=[jax.ShapeDtypeStruct(lat.shape, jnp.bfloat16)] + [face] * 6,
        in_specs=whole(1),
        out_specs=whole(7),
        scratch_shapes=[pltpu.VMEM((chan // 128, edge * plane, 128), jnp.float32)],
        compiler_params=pltpu.CompilerParams(vmem_limit_bytes=6 * MB),
        cost_estimate=pl.CostEstimate(flops=4 * MB, bytes_accessed=2 * MB, transcendentals=MB),
    )(lat)

    def shift(face, axis, step):
        count = lax.axis_size(axis)
        pairs = [(i, i + step) for i in range(count) if 0 <= i + step < count]
        return lax.ppermute(face, axis, pairs)

    far = (
        shift(zhi, "depth", 1),
        shift(zlo, "depth", -1),
        shift(yhi, "row", 1),
        shift(ylo, "row", -1),
        shift(xhi, "col", 1),
        shift(xlo, "col", -1),
    )
    x_got, z_got, far = lax.optimization_barrier((x_got, z_got, far))
    x_other = lax.ppermute(x_got, "row", swap)
    z_other = lax.ppermute(z_got, "row", swap)

    columns = pl.pallas_call(
        columns_kernel,
        out_shape=jax.ShapeDtypeStruct((10, slots, edge + 2, plane, chan), jnp.bfloat16),
        in_specs=[smem] + whole(13),
        out_specs=pl.BlockSpec(memory_space=VMEM),
        scratch_shapes=[
            pltpu.VMEM((6, 2 * slots + 1, plane, chan), jnp.bfloat16),
            pltpu.VMEM((2, plane, chan), jnp.float32),
            pltpu.VMEM((2, plane, chan), jnp.float32),
        ],
        compiler_params=pltpu.CompilerParams(vmem_limit_bytes=8 * MB),
        cost_estimate=pl.CostEstimate(flops=16 * MB, bytes_accessed=6 * MB, transcendentals=0),
    )(neighbours, fi, zlo, zhi, ylo, yhi, xlo, xhi, *far)

    send_cap = 2
    acc_shape = jax.ShapeDtypeStruct((slots, edge * plane, chan), jnp.float32)
    params = pltpu.CompilerParams(vmem_limit_bytes=10 * MB)
    acc = pl.pallas_call(
        own_kernel,
        out_shape=acc_shape,
        in_specs=whole(2),
        out_specs=pl.BlockSpec(memory_space=VMEM),
        compiler_params=params,
        cost_estimate=pl.CostEstimate(flops=1400 * MB, bytes_accessed=3 * MB, transcendentals=0),
    )(columns, own_w)
    acc = pl.pallas_call(
        side_kernel,
        out_shape=acc_shape,
        in_specs=whole(4),
        out_specs=pl.BlockSpec(memory_space=VMEM),
        compiler_params=params,
        cost_estimate=pl.CostEstimate(flops=2200 * MB, bytes_accessed=3 * MB, transcendentals=0),
    )(columns, x_got, z_got, acc)
    outgoing = pl.pallas_call(
        last_kernel,
        out_shape=jax.ShapeDtypeStruct((rows_n * send_cap, plane, chan), jnp.bfloat16),
        in_specs=[smem] + whole(6),
        out_specs=pl.BlockSpec(memory_space=VMEM),
        compiler_params=params,
        cost_estimate=pl.CostEstimate(flops=2000 * MB, bytes_accessed=3 * MB, transcendentals=0),
    )(owners, columns, x_other, z_other, lat, step_embed.reshape(1, chan), acc)

    arrived = lax.all_to_all(
        outgoing.reshape(rows_n, send_cap * plane, chan), "row", split_axis=0, concat_axis=0, tiled=True
    ).reshape(rows_n * send_cap, plane, chan)

    end = quarter * chan
    notes = own_w[::own_out, end : end + slots * 8].astype(jnp.int32)
    serial = jnp.arange(slots * 8, dtype=jnp.int32)
    before = serial[None, :] < serial[:, None]
    own_row = lax.axis_index("row")
    mine = (notes >= 0) & (notes // OCAP == own_row)
    again = jnp.any(mine[:, None, :] & before[None], axis=2)
    origin = jnp.arange(rows_n, dtype=jnp.int32)[:, None] * send_cap + again.astype(jnp.int32)
    wanted = jnp.arange(OCAP, dtype=jnp.int32)[:, None, None]
    source = jnp.sum(jnp.where(mine[None] & (notes[None] % OCAP == wanted), origin[None], 0), axis=(1, 2))

    half = edge // 2
    each = 4
    grown = pl.pallas_call(
        grow_kernel,
        grid_spec=pltpu.PrefetchScalarGridSpec(
            num_scalar_prefetch=1,
            grid=(OCAP // each,),
            in_specs=whole(2),
            out_specs=pl.BlockSpec((each, half, 2, half, 2, edge, co), lambda i, s: (i, 0, 0, 0, 0, 0, 0)),
            scratch_shapes=[pltpu.VMEM((each * plane * 2, co), jnp.float32)],
        ),
        out_shape=jax.ShapeDtypeStruct((OCAP, half, 2, half, 2, edge, co), jnp.bfloat16),
        compiler_params=pltpu.CompilerParams(vmem_limit_bytes=12 * MB),
        cost_estimate=pl.CostEstimate(flops=540 * MB, bytes_accessed=4 * MB, transcendentals=0),
    )(source, arrived, up_weight)
    return grown.reshape(1, 1, 1, OCAP, edge, edge, edge, co)


def solution(mesh):
    return jax.shard_map(
        body,
        mesh=mesh,
        in_specs=(
            P("depth", "row", "col", None, None, None, None, None),
            P("depth", "row", "col", None, None),
            P("depth", "row", "col", None, None),
            P(None, None, "row"),
            P(),
            P(),
        ),
        out_specs=P("depth", "row", "col", None, None, None, None, None),
        check_vma=False,
    )
```

```python
import jax
import jax.numpy as jnp
from jax import lax
from jax.experimental import pallas as pl
from jax.experimental.pallas import tpu as pltpu
from jax.sharding import PartitionSpec as P

OCAP = 16
VMEM = pltpu.VMEM
SMEM = pltpu.SMEM
MB = 1024 * 1024


def whole(count):
    return [pl.BlockSpec(memory_space=VMEM)] * count


def norm_kernel(lat_ref, fi_ref, faces_ref, give_ref, cross_ref, keep_ref, rows_ref):
    slots, edge, plane, _ = lat_ref.shape
    lanes = rows_ref.shape[-1]
    pieces = rows_ref.shape[0]
    for b in range(slots):
        for z in range(edge):
            v = lat_ref[b, z].astype(jnp.float32)
            mean_square = jnp.mean(v * v, axis=-1, keepdims=True)
            n = v * lax.rsqrt(mean_square + 1e-06)
            s = n / (1.0 + jnp.exp(-n))
            half = s.astype(jnp.bfloat16)
            fi_ref[b, z] = half
            if z == 0:
                faces_ref[1, b] = half
            if z == edge - 1:
                faces_ref[0, b] = half
            for p in range(pieces):
                rows_ref[p, pl.ds(z * plane, plane), :] = s[:, p * lanes : (p + 1) * lanes]
        for p in range(pieces):
            cols = pl.ds(p * lanes, lanes)
            low = rows_ref[p, pl.ds(0, plane, stride=edge), :]
            high = rows_ref[p, pl.ds(edge - 1, plane, stride=edge), :]
            faces_ref[5, b, :, cols] = low.astype(jnp.bfloat16)
            faces_ref[4, b, :, cols] = high.astype(jnp.bfloat16)
            low = [rows_ref[p, pl.ds(z * plane, edge), :] for z in range(edge)]
            faces_ref[3, b, :, cols] = jnp.concatenate(low, axis=0).astype(jnp.bfloat16)
            high = [rows_ref[p, pl.ds(z * plane + plane - edge, edge), :] for z in range(edge)]
            faces_ref[2, b, :, cols] = jnp.concatenate(high, axis=0).astype(jnp.bfloat16)
    core = core_here()
    for kind in range(2):
        keep_ref[kind] = faces_ref[4 * kind + core]
        give_ref[kind] = faces_ref[4 * kind + 1 - core]
    give_ref[2] = faces_ref[2 + core]
    cross_ref[...] = faces_ref[3 - core]


def pack_kernel(own_ref, keep_ref, met_ref, x_ref, z_ref):
    chan = keep_ref.shape[-1]
    face = keep_ref.shape[1] * keep_ref.shape[2]
    wide = x_ref.shape[1] - 2 * chan
    part = z_ref.shape[1] - 2 * chan
    x_ref[:, :wide] = own_ref[:, :wide]
    start = core_here() * ((wide - part) // chan) * chan
    z_ref[:, :part] = own_ref[:, pl.ds(pl.multiple_of(start, chan), part)]
    for kind, out_ref in ((0, x_ref), (1, z_ref)):
        left = out_ref.shape[1] - 2 * chan
        rest = out_ref.shape[0] - face
        out_ref[:face, left : left + chan] = keep_ref[kind].reshape(face, chan)
        out_ref[:face, left + chan :] = met_ref[kind].reshape(face, chan)
        out_ref[face:, left:] = jnp.zeros((rest, 2 * chan), jnp.bfloat16)


def quarter_kernel(owners_ref, weight_ref, out_ref):
    taps, rows, chan = weight_ref.shape
    count = out_ref.shape[1] // chan
    wide = out_ref.shape[1] - count * chan
    first = colour_here() * count
    lane = lax.broadcasted_iota(jnp.int32, (rows, wide), 1)
    note = jnp.zeros((rows, wide), jnp.int32)
    children = owners_ref.shape[-1]
    for i in range(owners_ref.shape[-2] * children):
        note = jnp.where(lane == i, owners_ref[0, 0, 0, i // children, i % children], note)
    for j in range(count):
        out_ref[:, j * chan : (j + 1) * chan] = weight_ref[jnp.minimum(first + j, taps - 1)]
    out_ref[:, count * chan :] = note.astype(jnp.float32).astype(jnp.bfloat16)


def columns_kernel(
    near_ref, fi_ref, faces_ref, met_ref, crossed_ref, x_ref, z_ref, xo_ref, zo_ref, out_ref, table_ref, ybuf_ref, xbuf_ref
):
    slots, edge, plane, chan = fi_ref.shape
    core = core_here()

    def ridden(ref, which):
        left = ref.shape[1] - (2 - which) * chan
        return ref[: slots * plane, left : left + chan].reshape(slots, plane, chan)

    far = pl.ds(slots, slots)
    for d in range(6):
        table_ref[d, 0:slots] = faces_ref[d]
        table_ref[d, 2 * slots] = jnp.zeros((plane, chan), jnp.bfloat16)
    table_ref[core, far] = ridden(x_ref, 0)
    table_ref[1 - core, far] = ridden(xo_ref, 1)
    table_ref[2 + core, far] = crossed_ref[...]
    table_ref[3 - core, far] = met_ref[2]
    table_ref[4 + core, far] = ridden(z_ref, 0)
    table_ref[5 - core, far] = ridden(zo_ref, 1)
    out_ref[9] = jnp.zeros(out_ref.shape[1:], jnp.bfloat16)
    at_x = lax.rem(lax.broadcasted_iota(jnp.int32, (plane + 2 * edge, chan), 0), edge)
    rows_n = lax.axis_size("row")
    cols_n = lax.axis_size("col")
    own = (lax.axis_index("depth") * rows_n + lax.axis_index("row")) * cols_n + lax.axis_index("col")
    steps = (-rows_n * cols_n, rows_n * cols_n, -cols_n, cols_n, -1, 1)

    def chosen(b, d):
        named = near_ref[0, 0, 0, b, d]
        here = named - own * slots
        there = named - (own + steps[d]) * slots
        is_here = (named >= 0) & (here >= 0) & (here < slots)
        is_there = (named >= 0) & (there >= 0) & (there < slots)
        index = jnp.where(is_here, here, jnp.where(is_there, slots + there, 2 * slots))
        return table_ref[d, index].astype(jnp.float32)

    def put(b, z, rows, left, right):
        zero = jnp.zeros((edge, chan), jnp.float32)

        def spread(halo):
            mid = jnp.broadcast_to(halo[:, None, :], (edge, edge, chan)).reshape(plane, chan)
            return jnp.concatenate([zero, mid, zero], axis=0)

        count = plane + 2 * edge
        moved = (
            jnp.where(at_x == 0, spread(left), pltpu.roll(rows, 1, 0)),
            rows,
            jnp.where(at_x == edge - 1, spread(right), pltpu.roll(rows, count - 1, 0)),
        )
        for dx in range(3):
            low, high = paired(moved[dx])
            for dy in range(3):
                out_ref[dy * 3 + dx, b, z] = octant_rows(low, high, dy).astype(jnp.bfloat16)

    def brick(b, _):
        zero = jnp.zeros((edge, chan), jnp.float32)
        for side in range(2):
            rows = jnp.concatenate([zero, chosen(b, side), zero], axis=0)
            put(b, side * (edge + 1), rows, zero, zero)
            ybuf_ref[side] = chosen(b, 2 + side)
            xbuf_ref[side] = chosen(b, 4 + side)

        def layer(z, _):
            strip = pl.ds(pl.multiple_of(z * edge, edge), edge)
            rows = jnp.concatenate(
                [ybuf_ref[0, strip, :], fi_ref[b, z].astype(jnp.float32), ybuf_ref[1, strip, :]], axis=0
            )
            put(b, z + 1, rows, xbuf_ref[0, strip, :], xbuf_ref[1, strip, :])
            return 0

        lax.fori_loop(0, edge, layer, 0)
        return 0

    lax.fori_loop(0, slots, brick, 0)


def paired(rows):
    edge = 8
    half = edge // 2
    lines = rows.shape[0] // edge
    in_low = lax.rem(lax.broadcasted_iota(jnp.int32, ((lines - 1) * edge, rows.shape[1]), 0), edge) < half
    turned = pltpu.roll(rows.reshape(lines, edge, -1), half, 1).reshape(rows.shape)
    first, second = slice(0, (lines - 1) * edge), slice(edge, lines * edge)
    low = jnp.where(in_low, rows[first], turned[second])
    high = jnp.where(in_low, turned[first], rows[second])
    return low, high


def octant_rows(low, high, start):
    edge = 8
    half = edge // 2
    out = []
    for ky in range(2):
        for side in (low, high):
            for y in range(0, half, 2):
                at = (ky * half + y + start) * edge
                out.append(side[at : at + edge])
    return jnp.concatenate(out, axis=0)


def colour_here():
    return lax.rem(lax.axis_index("depth") + 2 * lax.axis_index("col"), 4)


def core_here():
    return lax.rem(lax.axis_index("row"), 2)


def tap_rows(cols_ref, b, first, count):
    edge, plane, chan = cols_ref.shape[2] - 2, cols_ref.shape[3], cols_ref.shape[4]
    out = []
    for j in range(count):
        tap = first + j
        live = tap < 27
        which = jnp.where(live, lax.rem(tap, 9), 9)
        layer = jnp.where(live, lax.div(tap, 9), 0)
        out.append(cols_ref[which, b, pl.ds(layer, edge)].reshape(edge * plane, chan))
    return out


def times(lhs, weight):
    return lax.dot_general(
        jnp.concatenate(lhs, axis=1), weight, (((1,), (1,)), ((), ())), preferred_element_type=jnp.float32
    )


def own_kernel(cols_ref, own_ref, lat_ref, emb_ref, acc_ref):
    slots, edge, plane, chan = lat_ref.shape
    count = own_ref.shape[1] // chan
    first = colour_here() * count
    for b in range(slots):
        got = times(tap_rows(cols_ref, b, first, count), own_ref[:, : count * chan])
        acc_ref[b] = got + emb_ref[...]
        for z in range(edge):
            lat = lat_ref[b, z].astype(jnp.float32)
            low, high = paired(lat)
            acc_ref[b, z * plane : (z + 1) * plane] += octant_rows(low, high, 0)


def side_kernel(cols_ref, xw_ref, zw_ref, old_ref, acc_ref):
    chan = cols_ref.shape[4]
    count, part = xw_ref.shape[1] // chan - 2, zw_ref.shape[1] // chan - 2
    core, colour = core_here(), colour_here()
    x_first = lax.rem(colour + 3 + 2 * core, 4) * count
    z_first = lax.rem(colour + 2, 4) * count + core * (count - part)
    for b in range(acc_ref.shape[0]):
        got = times(tap_rows(cols_ref, b, x_first, count), xw_ref[:, : count * chan])
        got += times(tap_rows(cols_ref, b, z_first, part), zw_ref[:, : part * chan])
        acc_ref[b] = old_ref[b] + got


def last_kernel(owners_ref, cols_ref, xw_ref, zw_ref, old_ref, out_ref, stash_ref, sem):
    slots = old_ref.shape[0]
    edge, plane, chan = cols_ref.shape[2] - 2, cols_ref.shape[3], cols_ref.shape[4]
    half = edge // 2
    piece = half * half
    count, part = xw_ref.shape[1] // chan - 2, zw_ref.shape[1] // chan - 2
    rest = count - part
    core, colour = core_here(), colour_here()
    x_first = lax.rem(colour + 1 + 2 * core, 4) * count
    z_first = lax.rem(colour + 2, 4) * count + (1 - core) * part
    lanes = pl.ds(pl.multiple_of((1 - core) * (part - rest) * chan, chan), rest * chan)

    targets = [owners_ref[0, 0, 0, i // 8, i % 8] for i in range(slots * 8)]
    target_rows = [lax.shift_right_arithmetic(t, 4) for t in targets]
    spare = out_ref.shape[0]
    for b in range(slots):
        got = times(tap_rows(cols_ref, b, x_first, count), xw_ref[:, : count * chan])
        got += times(tap_rows(cols_ref, b, z_first, rest), zw_ref[:, lanes])
        refined = (old_ref[b] + got).astype(jnp.bfloat16)
        for k in range(8):
            i = b * 8 + k
            rank = 0
            for j in range(i):
                rank += (target_rows[j] == target_rows[i]).astype(jnp.int32)
            place = jnp.where(targets[i] >= 0, target_rows[i] * 2 + rank, spare)
            for z in range(half):
                at = ((k // 4) * half + z) * plane + (k % 4) * piece
                stash_ref[place, z * piece : (z + 1) * piece] = refined[at : at + piece]
    copy = pltpu.make_async_copy(stash_ref.at[pl.ds(0, spare)], out_ref, sem)
    copy.start()
    copy.wait()


def grow_kernel(source_ref, child_ref, up_ref, out_ref, rows_ref):
    step = pl.program_id(0)
    each = out_ref.shape[0]
    co = up_ref.shape[-1]
    voxels = child_ref.shape[1]
    lhs = jnp.concatenate([child_ref[source_ref[step * each + j]] for j in range(each)], axis=0)
    for pz in range(2):
        for py in range(2):
            p = pz * 4 + py * 2
            mats = jnp.concatenate([up_ref[p], up_ref[p + 1]], axis=1)
            res = jnp.dot(lhs, mats, preferred_element_type=jnp.float32)
            rows_ref[pl.ds(0, each * voxels, stride=2), :] = res[:, :co]
            rows_ref[pl.ds(1, each * voxels, stride=2), :] = res[:, co:]
            out_ref[:, :, pz, :, py] = (
                rows_ref[...].reshape(each, 4, 4, 8, co).astype(jnp.bfloat16)
            )


def body(latents, neighbours, owners, conv_weight, step_embed, up_weight):
    rows_n = lax.axis_size("row")
    cols_n = lax.axis_size("col")
    slots, edge, chan = latents.shape[3], latents.shape[4], latents.shape[-1]
    plane = edge * edge
    taps = conv_weight.shape[0]
    own_out = conv_weight.shape[2]
    co = up_weight.shape[-1]
    quarter = (taps + 1) // 4
    part = quarter // 2 + 1

    smem = pl.BlockSpec(memory_space=SMEM)
    piece = pl.pallas_call(
        quarter_kernel,
        out_shape=jax.ShapeDtypeStruct((own_out, quarter * chan + 128), jnp.bfloat16),
        in_specs=[smem] + whole(1),
        out_specs=pl.BlockSpec(memory_space=VMEM),
        compiler_params=pltpu.CompilerParams(vmem_limit_bytes=4 * MB),
    )(owners, conv_weight.transpose(0, 2, 1))
    lat = latents.reshape(slots, edge, plane, chan)
    def bf16(*shape):
        return jax.ShapeDtypeStruct(shape, jnp.bfloat16)

    fi, faces, give, cross, keep = pl.pallas_call(
        norm_kernel,
        out_shape=[
            bf16(*lat.shape),
            bf16(6, slots, plane, chan),
            bf16(3, slots, plane, chan),
            bf16(slots, plane, chan),
            bf16(2, slots, plane, chan),
        ],
        in_specs=whole(1),
        out_specs=whole(5),
        scratch_shapes=[pltpu.VMEM((chan // 128, edge * plane, 128), jnp.float32)],
        compiler_params=pltpu.CompilerParams(vmem_limit_bytes=6 * MB),
        cost_estimate=pl.CostEstimate(flops=4 * MB, bytes_accessed=2 * MB, transcendentals=MB),
    )(lat)
    swap = [(r, r ^ 1) for r in range(rows_n)]
    between = [(r, r + 1 - 2 * (1 - r % 2)) for r in range(1, rows_n - 1)]
    met = lax.ppermute(give, "row", swap)
    crossed = lax.ppermute(cross, "row", between)
    piece, met = lax.optimization_barrier((piece, met))
    own_w = lax.all_gather(piece, "row", axis=0, tiled=True)
    x_send, z_send = pl.pallas_call(
        pack_kernel,
        out_shape=[bf16(chan, (quarter + 2) * chan), bf16(chan, (part + 2) * chan)],
        in_specs=whole(3),
        out_specs=whole(2),
        compiler_params=pltpu.CompilerParams(vmem_limit_bytes=4 * MB),
        cost_estimate=pl.CostEstimate(flops=0, bytes_accessed=4 * MB, transcendentals=0),
    )(own_w, keep, met)
    depth_n = lax.axis_size("depth")
    x_pairs = [
        (d * rows_n + r, (d + 1 - 2 * (r % 2)) % depth_n * rows_n + r)
        for d in range(depth_n)
        for r in range(rows_n)
    ]
    z_pairs = [
        (r * cols_n + c, r * cols_n + (c + 1 - 2 * (r % 2)) % cols_n)
        for r in range(rows_n)
        for c in range(cols_n)
    ]
    x_got = lax.ppermute(x_send, ("depth", "row"), x_pairs)
    z_got = lax.ppermute(z_send, ("row", "col"), z_pairs)
    x_other = lax.ppermute(x_got, "row", swap)
    z_other = lax.ppermute(z_got, "row", swap)

    columns = pl.pallas_call(
        columns_kernel,
        out_shape=jax.ShapeDtypeStruct((10, slots, edge + 2, plane, chan), jnp.bfloat16),
        in_specs=[smem] + whole(8),
        out_specs=pl.BlockSpec(memory_space=VMEM),
        scratch_shapes=[
            pltpu.VMEM((6, 2 * slots + 1, plane, chan), jnp.bfloat16),
            pltpu.VMEM((2, plane, chan), jnp.float32),
            pltpu.VMEM((2, plane, chan), jnp.float32),
        ],
        compiler_params=pltpu.CompilerParams(vmem_limit_bytes=8 * MB),
        cost_estimate=pl.CostEstimate(flops=16 * MB, bytes_accessed=6 * MB, transcendentals=0),
    )(neighbours, fi, faces, met, crossed, x_got, z_got, x_other, z_other)

    send_cap = 2
    acc_shape = jax.ShapeDtypeStruct((slots, edge * plane, chan), jnp.float32)
    params = pltpu.CompilerParams(vmem_limit_bytes=10 * MB)
    acc = pl.pallas_call(
        own_kernel,
        out_shape=acc_shape,
        in_specs=whole(4),
        out_specs=pl.BlockSpec(memory_space=VMEM),
        compiler_params=params,
        cost_estimate=pl.CostEstimate(flops=1400 * MB, bytes_accessed=3 * MB, transcendentals=0),
    )(columns, own_w, lat, step_embed.reshape(1, chan))
    acc = pl.pallas_call(
        side_kernel,
        out_shape=acc_shape,
        in_specs=whole(4),
        out_specs=pl.BlockSpec(memory_space=VMEM),
        compiler_params=params,
        cost_estimate=pl.CostEstimate(flops=2200 * MB, bytes_accessed=3 * MB, transcendentals=0),
    )(columns, x_got, z_got, acc)
    outgoing = pl.pallas_call(
        last_kernel,
        out_shape=jax.ShapeDtypeStruct((rows_n * send_cap, plane, chan), jnp.bfloat16),
        in_specs=[smem] + whole(4),
        out_specs=pl.BlockSpec(memory_space=pl.ANY),
        scratch_shapes=[
            pltpu.VMEM((rows_n * send_cap + 1, plane, chan), jnp.bfloat16),
            pltpu.SemaphoreType.DMA,
        ],
        compiler_params=params,
        cost_estimate=pl.CostEstimate(flops=2000 * MB, bytes_accessed=3 * MB, transcendentals=0),
    )(owners, columns, x_other, z_other, acc)

    arrived = lax.all_to_all(
        outgoing.reshape(rows_n, send_cap * plane, chan), "row", split_axis=0, concat_axis=0, tiled=True
    ).reshape(rows_n * send_cap, plane, chan)

    end = quarter * chan
    notes = own_w[::own_out, end : end + slots * 8].astype(jnp.int32)
    serial = jnp.arange(slots * 8, dtype=jnp.int32)
    before = serial[None, :] < serial[:, None]
    own_row = lax.axis_index("row")
    mine = (notes >= 0) & (notes // OCAP == own_row)
    again = jnp.any(mine[:, None, :] & before[None], axis=2)
    origin = jnp.arange(rows_n, dtype=jnp.int32)[:, None] * send_cap + again.astype(jnp.int32)
    wanted = jnp.arange(OCAP, dtype=jnp.int32)[:, None, None]
    source = jnp.sum(jnp.where(mine[None] & (notes[None] % OCAP == wanted), origin[None], 0), axis=(1, 2))

    half = edge // 2
    each = 4
    grown = pl.pallas_call(
        grow_kernel,
        grid_spec=pltpu.PrefetchScalarGridSpec(
            num_scalar_prefetch=1,
            grid=(OCAP // each,),
            in_specs=whole(2),
            out_specs=pl.BlockSpec((each, half, 2, half, 2, edge, co), lambda i, s: (i, 0, 0, 0, 0, 0, 0)),
            scratch_shapes=[pltpu.VMEM((each * plane * 2, co), jnp.float32)],
        ),
        out_shape=jax.ShapeDtypeStruct((OCAP, half, 2, half, 2, edge, co), jnp.bfloat16),
        compiler_params=pltpu.CompilerParams(vmem_limit_bytes=12 * MB),
        cost_estimate=pl.CostEstimate(flops=540 * MB, bytes_accessed=4 * MB, transcendentals=0),
    )(source, arrived, up_weight)
    return grown.reshape(1, 1, 1, OCAP, edge, edge, edge, co)


def solution(mesh):
    return jax.shard_map(
        body,
        mesh=mesh,
        in_specs=(
            P("depth", "row", "col", None, None, None, None, None),
            P("depth", "row", "col", None, None),
            P("depth", "row", "col", None, None),
            P(None, None, "row"),
            P(),
            P(),
        ),
        out_specs=P("depth", "row", "col", None, None, None, None, None),
        check_vma=False,
    )
```

```python
import jax
import jax.numpy as jnp
from jax import lax
from jax.experimental import pallas as pl
from jax.experimental.pallas import tpu as pltpu
from jax.sharding import PartitionSpec as P

OCAP = 16
SHARE = 7
PART = 4
VMEM = pltpu.VMEM
SMEM = pltpu.SMEM
MB = 1024 * 1024


def whole(count):
    return [pl.BlockSpec(memory_space=VMEM)] * count


def norm_kernel(lat_ref, fi_ref, faces_ref, give_ref, cross_ref, keep_ref, rows_ref):
    slots, edge, plane, _ = lat_ref.shape
    lanes = rows_ref.shape[-1]
    pieces = rows_ref.shape[0]
    for b in range(slots):
        for z in range(edge):
            v = lat_ref[b, z].astype(jnp.float32)
            mean_square = jnp.mean(v * v, axis=-1, keepdims=True)
            n = v * lax.rsqrt(mean_square + 1e-06)
            s = n / (1.0 + jnp.exp(-n))
            half = s.astype(jnp.bfloat16)
            fi_ref[b, z] = half
            if z == 0:
                faces_ref[1, b] = half
            if z == edge - 1:
                faces_ref[0, b] = half
            for p in range(pieces):
                rows_ref[p, pl.ds(z * plane, plane), :] = s[:, p * lanes : (p + 1) * lanes]
        for p in range(pieces):
            cols = pl.ds(p * lanes, lanes)
            low = rows_ref[p, pl.ds(0, plane, stride=edge), :]
            high = rows_ref[p, pl.ds(edge - 1, plane, stride=edge), :]
            faces_ref[5, b, :, cols] = low.astype(jnp.bfloat16)
            faces_ref[4, b, :, cols] = high.astype(jnp.bfloat16)
            low = [rows_ref[p, pl.ds(z * plane, edge), :] for z in range(edge)]
            faces_ref[3, b, :, cols] = jnp.concatenate(low, axis=0).astype(jnp.bfloat16)
            high = [rows_ref[p, pl.ds(z * plane + plane - edge, edge), :] for z in range(edge)]
            faces_ref[2, b, :, cols] = jnp.concatenate(high, axis=0).astype(jnp.bfloat16)
    core = core_here()
    for kind in range(2):
        keep_ref[kind] = faces_ref[4 * kind + core]
        give_ref[kind] = faces_ref[4 * kind + 1 - core]
    give_ref[2] = faces_ref[2 + core]
    cross_ref[...] = faces_ref[3 - core]


def pack_kernel(own_ref, keep_ref, met_ref, x_ref, z_ref):
    chan = keep_ref.shape[-1]
    lanes = chan // 2
    face = keep_ref.shape[1] * keep_ref.shape[2]
    full, some = SHARE * lanes, PART * lanes
    left = full + some
    for kind, out_ref in ((0, x_ref), (1, z_ref)):
        start = (1 - kind) * full + core_here() * (full - some)
        rest = out_ref.shape[0] - face
        out_ref[:, :full] = own_ref[:, kind * full : (kind + 1) * full]
        out_ref[:, full:left] = own_ref[:, pl.ds(pl.multiple_of(start, lanes), some)]
        out_ref[:face, left : left + chan] = keep_ref[kind].reshape(face, chan)
        out_ref[:face, left + chan :] = met_ref[kind].reshape(face, chan)
        out_ref[face:, left:] = jnp.zeros((rest, 2 * chan), jnp.bfloat16)


def quarter_kernel(owners_ref, weight_ref, out_ref):
    taps, rows, chan = weight_ref.shape
    lanes = chan // 2
    children = owners_ref.shape[-1]
    lane = lax.broadcasted_iota(jnp.int32, (rows, lanes), 1)
    note = jnp.zeros((rows, lanes), jnp.int32)
    for i in range(owners_ref.shape[-2] * children):
        note = jnp.where(lane == i, owners_ref[0, 0, 0, i // children, i % children], note)
    out_ref[:, 2 * SHARE * lanes :] = note.astype(jnp.float32).astype(jnp.bfloat16)
    for half in range(2):
        first = half * 4 * SHARE + colours()[half] * SHARE
        for j in range(SHARE):
            unit = first + j
            taken = weight_ref[jnp.minimum(lax.div(unit, 2), taps - 1)]
            odd = lax.rem(unit, 2) == 1
            at = (half * SHARE + j) * lanes
            out_ref[:, at : at + lanes] = jnp.where(odd, taken[:, lanes:], taken[:, :lanes])


def columns_kernel(
    near_ref, fi_ref, faces_ref, met_ref, crossed_ref, x_ref, z_ref, xo_ref, zo_ref, out_ref, table_ref, ybuf_ref, xbuf_ref
):
    slots, edge, plane, chan = fi_ref.shape
    core = core_here()

    def ridden(ref, which):
        left = ref.shape[1] - (2 - which) * chan
        return ref[: slots * plane, left : left + chan].reshape(slots, plane, chan)

    far = pl.ds(slots, slots)
    for d in range(6):
        table_ref[d, 0:slots] = faces_ref[d]
        table_ref[d, 2 * slots] = jnp.zeros((plane, chan), jnp.bfloat16)
    table_ref[core, far] = ridden(x_ref, 0)
    table_ref[1 - core, far] = ridden(xo_ref, 1)
    table_ref[2 + core, far] = crossed_ref[...]
    table_ref[3 - core, far] = met_ref[2]
    table_ref[4 + core, far] = ridden(z_ref, 0)
    table_ref[5 - core, far] = ridden(zo_ref, 1)
    out_ref[18] = jnp.zeros(out_ref.shape[1:], jnp.bfloat16)
    at_x = lax.rem(lax.broadcasted_iota(jnp.int32, (plane + 2 * edge, chan), 0), edge)
    rows_n = lax.axis_size("row")
    cols_n = lax.axis_size("col")
    own = (lax.axis_index("depth") * rows_n + lax.axis_index("row")) * cols_n + lax.axis_index("col")
    steps = (-rows_n * cols_n, rows_n * cols_n, -cols_n, cols_n, -1, 1)

    def chosen(b, d):
        named = near_ref[0, 0, 0, b, d]
        here = named - own * slots
        there = named - (own + steps[d]) * slots
        is_here = (named >= 0) & (here >= 0) & (here < slots)
        is_there = (named >= 0) & (there >= 0) & (there < slots)
        index = jnp.where(is_here, here, jnp.where(is_there, slots + there, 2 * slots))
        return table_ref[d, index].astype(jnp.float32)

    def put(b, z, rows, left, right):
        zero = jnp.zeros((edge, chan), jnp.float32)

        def spread(halo):
            mid = jnp.broadcast_to(halo[:, None, :], (edge, edge, chan)).reshape(plane, chan)
            return jnp.concatenate([zero, mid, zero], axis=0)

        count = plane + 2 * edge
        moved = (
            jnp.where(at_x == 0, spread(left), pltpu.roll(rows, 1, 0)),
            rows,
            jnp.where(at_x == edge - 1, spread(right), pltpu.roll(rows, count - 1, 0)),
        )
        for dx in range(3):
            low, high = paired(moved[dx])
            for dy in range(3):
                full = octant_rows(low, high, dy).astype(jnp.bfloat16)
                unit = (dy * 3 + dx) * 2
                out_ref[unit, b, z] = full[:, : chan // 2]
                out_ref[unit + 1, b, z] = full[:, chan // 2 :]

    def brick(b, _):
        zero = jnp.zeros((edge, chan), jnp.float32)
        for side in range(2):
            rows = jnp.concatenate([zero, chosen(b, side), zero], axis=0)
            put(b, side * (edge + 1), rows, zero, zero)
            ybuf_ref[side] = chosen(b, 2 + side)
            xbuf_ref[side] = chosen(b, 4 + side)

        def layer(z, _):
            strip = pl.ds(pl.multiple_of(z * edge, edge), edge)
            rows = jnp.concatenate(
                [ybuf_ref[0, strip, :], fi_ref[b, z].astype(jnp.float32), ybuf_ref[1, strip, :]], axis=0
            )
            put(b, z + 1, rows, xbuf_ref[0, strip, :], xbuf_ref[1, strip, :])
            return 0

        lax.fori_loop(0, edge, layer, 0)
        return 0

    lax.fori_loop(0, slots, brick, 0)


def paired(rows):
    edge = 8
    half = edge // 2
    lines = rows.shape[0] // edge
    in_low = lax.rem(lax.broadcasted_iota(jnp.int32, ((lines - 1) * edge, rows.shape[1]), 0), edge) < half
    turned = pltpu.roll(rows.reshape(lines, edge, -1), half, 1).reshape(rows.shape)
    first, second = slice(0, (lines - 1) * edge), slice(edge, lines * edge)
    low = jnp.where(in_low, rows[first], turned[second])
    high = jnp.where(in_low, turned[first], rows[second])
    return low, high


def octant_rows(low, high, start):
    edge = 8
    half = edge // 2
    out = []
    for ky in range(2):
        for side in (low, high):
            for y in range(0, half, 2):
                at = (ky * half + y + start) * edge
                out.append(side[at : at + edge])
    return jnp.concatenate(out, axis=0)


def colours():
    depth, col = lax.axis_index("depth"), lax.axis_index("col")
    return lax.rem(depth + 2 * col, 4), lax.rem(col + 2 * depth, 4)


def core_here():
    return lax.rem(lax.axis_index("row"), 2)


def unit_rows(cols_ref, b, first, count):
    edge, plane, lanes = cols_ref.shape[2] - 2, cols_ref.shape[3], cols_ref.shape[4]
    out = []
    for j in range(count):
        unit = first + j
        live = unit < 54
        which = jnp.where(live, lax.rem(unit, 18), 18)
        layer = jnp.where(live, lax.div(unit, 18), 0)
        out.append(cols_ref[which, b, pl.ds(layer, edge)].reshape(edge * plane, lanes))
    return out


def conv_kernel(
    owners_ref, cols_ref, own_ref, x_ref, z_ref, xo_ref, zo_ref, lat_ref, emb_ref, out_ref, stash_ref, sem
):
    slots, edge, plane, chan = lat_ref.shape
    lanes = cols_ref.shape[4]
    half = edge // 2
    piece = half * half
    core = core_here()
    full, some, rest = SHARE * lanes, PART * lanes, (SHARE - PART) * lanes
    spans = []
    weights = [own_ref[:, : 2 * full]]
    for kind, colour in enumerate(colours()):
        spans.append((kind * 4 * SHARE + colour * SHARE, SHARE))
    late = pl.ds(pl.multiple_of(full + (1 - core) * (some - rest), lanes), rest)
    for kind, got_ref, other_ref in ((0, x_ref, xo_ref), (1, z_ref, zo_ref)):
        near = kind * 4 * SHARE
        cross = (1 - kind) * 4 * SHARE + lax.rem(colours()[1 - kind] + 2, 4) * SHARE
        colour = colours()[kind]
        spans.append((near + lax.rem(colour + 3 + 2 * core, 4) * SHARE, SHARE))
        spans.append((cross + core * (SHARE - PART), PART))
        spans.append((near + lax.rem(colour + 1 + 2 * core, 4) * SHARE, SHARE))
        spans.append((cross + (1 - core) * PART, SHARE - PART))
        weights += [got_ref[:, : full + some], other_ref[:, :full], other_ref[:, late]]
    weight = jnp.concatenate(weights, axis=1)

    targets = [owners_ref[0, 0, 0, i // 8, i % 8] for i in range(slots * 8)]
    target_rows = [lax.shift_right_arithmetic(t, 4) for t in targets]
    spare = out_ref.shape[0]
    for b in range(slots):
        rows = []
        for first, count in spans:
            rows += unit_rows(cols_ref, b, first, count)
        total = lax.dot_general(
            jnp.concatenate(rows, axis=1), weight, (((1,), (1,)), ((), ())), preferred_element_type=jnp.float32
        )
        total += emb_ref[...]
        places = []
        for k in range(8):
            i = b * 8 + k
            rank = 0
            for j in range(i):
                rank += (target_rows[j] == target_rows[i]).astype(jnp.int32)
            places.append(jnp.where(targets[i] >= 0, target_rows[i] * 2 + rank, spare))
        for z in range(edge):
            low, high = paired(lat_ref[b, z].astype(jnp.float32))
            refined = total[z * plane : (z + 1) * plane] + octant_rows(low, high, 0)
            refined = refined.astype(jnp.bfloat16)
            at = (z % half) * piece
            for side in range(4):
                stash_ref[places[z // half * 4 + side], at : at + piece] = refined[
                    side * piece : (side + 1) * piece
                ]
    copy = pltpu.make_async_copy(stash_ref.at[pl.ds(0, spare)], out_ref, sem)
    copy.start()
    copy.wait()


def grow_kernel(source_ref, child_ref, up_ref, out_ref, rows_ref):
    step = pl.program_id(0)
    each = out_ref.shape[0]
    co = up_ref.shape[-1]
    voxels = child_ref.shape[1]
    lhs = jnp.concatenate([child_ref[source_ref[step * each + j]] for j in range(each)], axis=0)
    for pz in range(2):
        for py in range(2):
            p = pz * 4 + py * 2
            mats = jnp.concatenate([up_ref[p], up_ref[p + 1]], axis=1)
            res = jnp.dot(lhs, mats, preferred_element_type=jnp.float32)
            rows_ref[pl.ds(0, each * voxels, stride=2), :] = res[:, :co]
            rows_ref[pl.ds(1, each * voxels, stride=2), :] = res[:, co:]
            out_ref[:, :, pz, :, py] = (
                rows_ref[...].reshape(each, 4, 4, 8, co).astype(jnp.bfloat16)
            )


def body(latents, neighbours, owners, conv_weight, step_embed, up_weight):
    rows_n = lax.axis_size("row")
    cols_n = lax.axis_size("col")
    slots, edge, chan = latents.shape[3], latents.shape[4], latents.shape[-1]
    plane = edge * edge
    own_out = conv_weight.shape[2]
    co = up_weight.shape[-1]
    smem = pl.BlockSpec(memory_space=SMEM)
    piece = pl.pallas_call(
        quarter_kernel,
        out_shape=jax.ShapeDtypeStruct((own_out, SHARE * chan + chan // 2), jnp.bfloat16),
        in_specs=[smem] + whole(1),
        out_specs=pl.BlockSpec(memory_space=VMEM),
        compiler_params=pltpu.CompilerParams(vmem_limit_bytes=4 * MB),
    )(owners, conv_weight.transpose(0, 2, 1))
    lat = latents.reshape(slots, edge, plane, chan)
    def bf16(*shape):
        return jax.ShapeDtypeStruct(shape, jnp.bfloat16)

    fi, faces, give, cross, keep = pl.pallas_call(
        norm_kernel,
        out_shape=[
            bf16(*lat.shape),
            bf16(6, slots, plane, chan),
            bf16(3, slots, plane, chan),
            bf16(slots, plane, chan),
            bf16(2, slots, plane, chan),
        ],
        in_specs=whole(1),
        out_specs=whole(5),
        scratch_shapes=[pltpu.VMEM((chan // 128, edge * plane, 128), jnp.float32)],
        compiler_params=pltpu.CompilerParams(vmem_limit_bytes=6 * MB),
        cost_estimate=pl.CostEstimate(flops=4 * MB, bytes_accessed=2 * MB, transcendentals=MB),
    )(lat)
    swap = [(r, r ^ 1) for r in range(rows_n)]
    between = [(r, r + 1 - 2 * (1 - r % 2)) for r in range(1, rows_n - 1)]
    met = lax.ppermute(give, "row", swap)
    crossed = lax.ppermute(cross, "row", between)
    piece, met = lax.optimization_barrier((piece, met))
    own_w = lax.all_gather(piece, "row", axis=0, tiled=True)
    x_send, z_send = pl.pallas_call(
        pack_kernel,
        out_shape=[bf16(chan, (SHARE + PART) * chan // 2 + 2 * chan)] * 2,
        in_specs=whole(3),
        out_specs=whole(2),
        compiler_params=pltpu.CompilerParams(vmem_limit_bytes=4 * MB),
        cost_estimate=pl.CostEstimate(flops=0, bytes_accessed=4 * MB, transcendentals=0),
    )(own_w, keep, met)
    depth_n = lax.axis_size("depth")
    x_pairs = [
        (d * rows_n + r, (d + 1 - 2 * (r % 2)) % depth_n * rows_n + r)
        for d in range(depth_n)
        for r in range(rows_n)
    ]
    z_pairs = [
        (r * cols_n + c, r * cols_n + (c + 1 - 2 * (r % 2)) % cols_n)
        for r in range(rows_n)
        for c in range(cols_n)
    ]
    x_got = lax.ppermute(x_send, ("depth", "row"), x_pairs)
    z_got = lax.ppermute(z_send, ("row", "col"), z_pairs)
    x_got, crossed = lax.optimization_barrier((x_got, crossed))
    x_other = lax.ppermute(x_got, "row", swap)
    z_other = lax.ppermute(z_got, "row", swap)

    columns = pl.pallas_call(
        columns_kernel,
        out_shape=bf16(19, slots, edge + 2, plane, chan // 2),
        in_specs=[smem] + whole(8),
        out_specs=pl.BlockSpec(memory_space=VMEM),
        scratch_shapes=[
            pltpu.VMEM((6, 2 * slots + 1, plane, chan), jnp.bfloat16),
            pltpu.VMEM((2, plane, chan), jnp.float32),
            pltpu.VMEM((2, plane, chan), jnp.float32),
        ],
        compiler_params=pltpu.CompilerParams(vmem_limit_bytes=8 * MB),
        cost_estimate=pl.CostEstimate(flops=16 * MB, bytes_accessed=6 * MB, transcendentals=0),
    )(neighbours, fi, faces, met, crossed, x_got, z_got, x_other, z_other)

    send_cap = 2
    outgoing = pl.pallas_call(
        conv_kernel,
        out_shape=bf16(rows_n * send_cap, plane, chan),
        in_specs=[smem] + whole(8),
        out_specs=pl.BlockSpec(memory_space=pl.ANY),
        scratch_shapes=[
            pltpu.VMEM((rows_n * send_cap + 1, plane, chan), jnp.bfloat16),
            pltpu.SemaphoreType.DMA,
        ],
        compiler_params=pltpu.CompilerParams(vmem_limit_bytes=26 * MB),
        cost_estimate=pl.CostEstimate(flops=5600 * MB, bytes_accessed=8 * MB, transcendentals=0),
    )(owners, columns, own_w, x_got, z_got, x_other, z_other, lat, step_embed.reshape(1, chan))

    arrived = lax.all_to_all(
        outgoing.reshape(rows_n, send_cap * plane, chan), "row", split_axis=0, concat_axis=0, tiled=True
    ).reshape(rows_n * send_cap, plane, chan)

    end = SHARE * chan
    notes = own_w[::own_out, end : end + slots * 8].astype(jnp.int32)
    serial = jnp.arange(slots * 8, dtype=jnp.int32)
    before = serial[None, :] < serial[:, None]
    own_row = lax.axis_index("row")
    mine = (notes >= 0) & (notes // OCAP == own_row)
    again = jnp.any(mine[:, None, :] & before[None], axis=2)
    origin = jnp.arange(rows_n, dtype=jnp.int32)[:, None] * send_cap + again.astype(jnp.int32)
    wanted = jnp.arange(OCAP, dtype=jnp.int32)[:, None, None]
    source = jnp.sum(jnp.where(mine[None] & (notes[None] % OCAP == wanted), origin[None], 0), axis=(1, 2))

    half = edge // 2
    each = 4
    grown = pl.pallas_call(
        grow_kernel,
        grid_spec=pltpu.PrefetchScalarGridSpec(
            num_scalar_prefetch=1,
            grid=(OCAP // each,),
            in_specs=whole(2),
            out_specs=pl.BlockSpec((each, half, 2, half, 2, edge, co), lambda i, s: (i, 0, 0, 0, 0, 0, 0)),
            scratch_shapes=[pltpu.VMEM((each * plane * 2, co), jnp.float32)],
        ),
        out_shape=jax.ShapeDtypeStruct((OCAP, half, 2, half, 2, edge, co), jnp.bfloat16),
        compiler_params=pltpu.CompilerParams(vmem_limit_bytes=12 * MB),
        cost_estimate=pl.CostEstimate(flops=540 * MB, bytes_accessed=4 * MB, transcendentals=0),
    )(source, arrived, up_weight)
    return grown.reshape(1, 1, 1, OCAP, edge, edge, edge, co)


def solution(mesh):
    return jax.shard_map(
        body,
        mesh=mesh,
        in_specs=(
            P("depth", "row", "col", None, None, None, None, None),
            P("depth", "row", "col", None, None),
            P("depth", "row", "col", None, None),
            P(None, None, "row"),
            P(),
            P(),
        ),
        out_specs=P("depth", "row", "col", None, None, None, None, None),
        check_vma=False,
    )
```

```python
import jax
import jax.numpy as jnp
from jax import lax
from jax.experimental import pallas as pl
from jax.experimental.pallas import tpu as pltpu
from jax.sharding import PartitionSpec as P

OCAP = 16
SHARE = 7
PART = 4
VMEM = pltpu.VMEM
SMEM = pltpu.SMEM
MB = 1024 * 1024


def whole(count):
    return [pl.BlockSpec(memory_space=VMEM)] * count


def norm_kernel(lat_ref, fi_ref, faces_ref, give_ref, cross_ref, keep_ref, rows_ref):
    slots, edge, plane, _ = lat_ref.shape
    lanes = rows_ref.shape[-1]
    pieces = rows_ref.shape[0]
    for b in range(slots):
        for z in range(edge):
            v = lat_ref[b, z].astype(jnp.float32)
            mean_square = jnp.mean(v * v, axis=-1, keepdims=True)
            n = v * lax.rsqrt(mean_square + 1e-06)
            s = n / (1.0 + jnp.exp(-n))
            half = s.astype(jnp.bfloat16)
            fi_ref[b, z] = half
            if z == 0:
                faces_ref[1, b] = half
            if z == edge - 1:
                faces_ref[0, b] = half
            for p in range(pieces):
                rows_ref[p, pl.ds(z * plane, plane), :] = s[:, p * lanes : (p + 1) * lanes]
        for p in range(pieces):
            cols = pl.ds(p * lanes, lanes)
            low = rows_ref[p, pl.ds(0, plane, stride=edge), :]
            high = rows_ref[p, pl.ds(edge - 1, plane, stride=edge), :]
            faces_ref[5, b, :, cols] = low.astype(jnp.bfloat16)
            faces_ref[4, b, :, cols] = high.astype(jnp.bfloat16)
            low = [rows_ref[p, pl.ds(z * plane, edge), :] for z in range(edge)]
            faces_ref[3, b, :, cols] = jnp.concatenate(low, axis=0).astype(jnp.bfloat16)
            high = [rows_ref[p, pl.ds(z * plane + plane - edge, edge), :] for z in range(edge)]
            faces_ref[2, b, :, cols] = jnp.concatenate(high, axis=0).astype(jnp.bfloat16)
    core = core_here()
    for kind in range(2):
        keep_ref[kind] = faces_ref[4 * kind + core]
        give_ref[kind] = faces_ref[4 * kind + 1 - core]
    give_ref[2] = faces_ref[2 + core]
    cross_ref[...] = faces_ref[3 - core]


def pack_kernel(own_ref, keep_ref, met_ref, x_ref, z_ref):
    chan = keep_ref.shape[-1]
    lanes = chan // 2
    face = keep_ref.shape[1] * keep_ref.shape[2]
    full, some = SHARE * lanes, PART * lanes
    left = full + some
    for kind, out_ref in ((0, x_ref), (1, z_ref)):
        start = (1 - kind) * full + core_here() * (full - some)
        rest = out_ref.shape[0] - face
        out_ref[:, :full] = own_ref[:, kind * full : (kind + 1) * full]
        out_ref[:, full:left] = own_ref[:, pl.ds(pl.multiple_of(start, lanes), some)]
        out_ref[:face, left : left + chan] = keep_ref[kind].reshape(face, chan)
        out_ref[:face, left + chan :] = met_ref[kind].reshape(face, chan)
        out_ref[face:, left:] = jnp.zeros((rest, 2 * chan), jnp.bfloat16)


def quarter_kernel(owners_ref, weight_ref, out_ref):
    taps, rows, chan = weight_ref.shape
    lanes = chan // 2
    children = owners_ref.shape[-1]
    lane = lax.broadcasted_iota(jnp.int32, (rows, lanes), 1)
    note = jnp.zeros((rows, lanes), jnp.int32)
    for i in range(owners_ref.shape[-2] * children):
        note = jnp.where(lane == i, owners_ref[0, 0, 0, i // children, i % children], note)
    out_ref[:, 2 * SHARE * lanes :] = note.astype(jnp.float32).astype(jnp.bfloat16)
    for half in range(2):
        first = half * 4 * SHARE + colours()[half] * SHARE
        for j in range(SHARE):
            unit = first + j
            taken = weight_ref[jnp.minimum(lax.div(unit, 2), taps - 1)]
            odd = lax.rem(unit, 2) == 1
            at = (half * SHARE + j) * lanes
            out_ref[:, at : at + lanes] = jnp.where(odd, taken[:, lanes:], taken[:, :lanes])


def columns_kernel(
    near_ref, fi_ref, faces_ref, met_ref, crossed_ref, x_ref, z_ref, xo_ref, zo_ref, out_ref, table_ref, ybuf_ref, xbuf_ref
):
    slots, edge, plane, chan = fi_ref.shape
    core = core_here()

    def ridden(ref, which):
        left = ref.shape[1] - (2 - which) * chan
        return ref[: slots * plane, left : left + chan].reshape(slots, plane, chan)

    far = pl.ds(slots, slots)
    for d in range(6):
        table_ref[d, 0:slots] = faces_ref[d]
        table_ref[d, 2 * slots] = jnp.zeros((plane, chan), jnp.bfloat16)
    table_ref[core, far] = ridden(x_ref, 0)
    table_ref[1 - core, far] = ridden(xo_ref, 1)
    table_ref[2 + core, far] = crossed_ref[...]
    table_ref[3 - core, far] = met_ref[2]
    table_ref[4 + core, far] = ridden(z_ref, 0)
    table_ref[5 - core, far] = ridden(zo_ref, 1)
    out_ref[18] = jnp.zeros(out_ref.shape[1:], jnp.bfloat16)
    at_x = lax.rem(lax.broadcasted_iota(jnp.int32, (plane + 2 * edge, chan), 0), edge)
    rows_n = lax.axis_size("row")
    cols_n = lax.axis_size("col")
    own = (lax.axis_index("depth") * rows_n + lax.axis_index("row")) * cols_n + lax.axis_index("col")
    steps = (-rows_n * cols_n, rows_n * cols_n, -cols_n, cols_n, -1, 1)

    def chosen(b, d):
        named = near_ref[0, 0, 0, b, d]
        here = named - own * slots
        there = named - (own + steps[d]) * slots
        is_here = (named >= 0) & (here >= 0) & (here < slots)
        is_there = (named >= 0) & (there >= 0) & (there < slots)
        index = jnp.where(is_here, here, jnp.where(is_there, slots + there, 2 * slots))
        return table_ref[d, index].astype(jnp.float32)

    def put(b, z, rows, left, right):
        zero = jnp.zeros((edge, chan), jnp.float32)

        def spread(halo):
            mid = jnp.broadcast_to(halo[:, None, :], (edge, edge, chan)).reshape(plane, chan)
            return jnp.concatenate([zero, mid, zero], axis=0)

        count = plane + 2 * edge
        moved = (
            jnp.where(at_x == 0, spread(left), pltpu.roll(rows, 1, 0)),
            rows,
            jnp.where(at_x == edge - 1, spread(right), pltpu.roll(rows, count - 1, 0)),
        )
        for dx in range(3):
            low, high = paired(moved[dx])
            for dy in range(3):
                full = octant_rows(low, high, dy).astype(jnp.bfloat16)
                unit = (dy * 3 + dx) * 2
                out_ref[unit, b, z] = full[:, : chan // 2]
                out_ref[unit + 1, b, z] = full[:, chan // 2 :]

    def brick(b, _):
        zero = jnp.zeros((edge, chan), jnp.float32)
        for side in range(2):
            rows = jnp.concatenate([zero, chosen(b, side), zero], axis=0)
            put(b, side * (edge + 1), rows, zero, zero)
            ybuf_ref[side] = chosen(b, 2 + side)
            xbuf_ref[side] = chosen(b, 4 + side)

        def layer(z, _):
            strip = pl.ds(pl.multiple_of(z * edge, edge), edge)
            rows = jnp.concatenate(
                [ybuf_ref[0, strip, :], fi_ref[b, z].astype(jnp.float32), ybuf_ref[1, strip, :]], axis=0
            )
            put(b, z + 1, rows, xbuf_ref[0, strip, :], xbuf_ref[1, strip, :])
            return 0

        lax.fori_loop(0, edge, layer, 0)
        return 0

    lax.fori_loop(0, slots, brick, 0)


def paired(rows):
    edge = 8
    half = edge // 2
    lines = rows.shape[0] // edge
    in_low = lax.rem(lax.broadcasted_iota(jnp.int32, ((lines - 1) * edge, rows.shape[1]), 0), edge) < half
    turned = pltpu.roll(rows.reshape(lines, edge, -1), half, 1).reshape(rows.shape)
    first, second = slice(0, (lines - 1) * edge), slice(edge, lines * edge)
    low = jnp.where(in_low, rows[first], turned[second])
    high = jnp.where(in_low, turned[first], rows[second])
    return low, high


def octant_rows(low, high, start):
    edge = 8
    half = edge // 2
    out = []
    for ky in range(2):
        for side in (low, high):
            for y in range(0, half, 2):
                at = (ky * half + y + start) * edge
                out.append(side[at : at + edge])
    return jnp.concatenate(out, axis=0)


def colours():
    depth, col = lax.axis_index("depth"), lax.axis_index("col")
    return lax.rem(depth + 2 * col, 4), lax.rem(col + 2 * depth, 4)


def core_here():
    return lax.rem(lax.axis_index("row"), 2)


def unit_rows(cols_ref, b, first, count):
    edge, plane, lanes = cols_ref.shape[2] - 2, cols_ref.shape[3], cols_ref.shape[4]
    out = []
    for j in range(count):
        unit = first + j
        live = unit < 54
        which = jnp.where(live, lax.rem(unit, 18), 18)
        layer = jnp.where(live, lax.div(unit, 18), 0)
        out.append(cols_ref[which, b, pl.ds(layer, edge)].reshape(edge * plane, lanes))
    return out


def conv_kernel(
    owners_ref, cols_ref, own_ref, x_ref, z_ref, xo_ref, zo_ref, lat_ref, emb_ref, out_ref, stash_ref, sem
):
    slots, edge, plane, chan = lat_ref.shape
    lanes = cols_ref.shape[4]
    half = edge // 2
    piece = half * half
    core = core_here()
    full, some, rest = SHARE * lanes, PART * lanes, (SHARE - PART) * lanes
    spans = []
    weights = [own_ref[:, : 2 * full]]
    for kind, colour in enumerate(colours()):
        spans.append((kind * 4 * SHARE + colour * SHARE, SHARE))
    late = pl.ds(pl.multiple_of(full + (1 - core) * (some - rest), lanes), rest)
    for kind, got_ref, other_ref in ((0, x_ref, xo_ref), (1, z_ref, zo_ref)):
        near = kind * 4 * SHARE
        cross = (1 - kind) * 4 * SHARE + lax.rem(colours()[1 - kind] + 2, 4) * SHARE
        colour = colours()[kind]
        spans.append((near + lax.rem(colour + 3 + 2 * core, 4) * SHARE, SHARE))
        spans.append((cross + core * (SHARE - PART), PART))
        spans.append((near + lax.rem(colour + 1 + 2 * core, 4) * SHARE, SHARE))
        spans.append((cross + (1 - core) * PART, SHARE - PART))
        weights += [got_ref[:, : full + some], other_ref[:, :full], other_ref[:, late]]
    weight = jnp.concatenate(weights, axis=1)

    targets = [owners_ref[0, 0, 0, i // 8, i % 8] for i in range(slots * 8)]
    target_rows = [lax.shift_right_arithmetic(t, 4) for t in targets]
    spare = out_ref.shape[0]
    for b in range(slots):
        rows = []
        for first, count in spans:
            rows += unit_rows(cols_ref, b, first, count)
        total = lax.dot_general(
            jnp.concatenate(rows, axis=1), weight, (((1,), (1,)), ((), ())), preferred_element_type=jnp.float32
        )
        total += emb_ref[...]
        places = []
        for k in range(8):
            i = b * 8 + k
            rank = 0
            for j in range(i):
                rank += (target_rows[j] == target_rows[i]).astype(jnp.int32)
            places.append(jnp.where(targets[i] >= 0, target_rows[i] * 2 + rank, spare))
        for z in range(edge):
            low, high = paired(lat_ref[b, z].astype(jnp.float32))
            refined = total[z * plane : (z + 1) * plane] + octant_rows(low, high, 0)
            refined = refined.astype(jnp.bfloat16)
            at = (z % half) * piece
            for side in range(4):
                stash_ref[places[z // half * 4 + side], at : at + piece] = refined[
                    side * piece : (side + 1) * piece
                ]
    copy = pltpu.make_async_copy(stash_ref.at[pl.ds(0, spare)], out_ref, sem)
    copy.start()
    copy.wait()


def grow_kernel(source_ref, child_ref, up_ref, out_ref, rows_ref):
    step = pl.program_id(0)
    each = out_ref.shape[0]
    co = up_ref.shape[-1]
    voxels = child_ref.shape[1]
    lhs = jnp.concatenate([child_ref[source_ref[step * each + j]] for j in range(each)], axis=0)
    for pz in range(2):
        for py in range(2):
            p = pz * 4 + py * 2
            mats = jnp.concatenate([up_ref[p], up_ref[p + 1]], axis=1)
            res = jnp.dot(lhs, mats, preferred_element_type=jnp.float32)
            rows_ref[pl.ds(0, each * voxels, stride=2), :] = res[:, :co]
            rows_ref[pl.ds(1, each * voxels, stride=2), :] = res[:, co:]
            out_ref[:, :, pz, :, py] = (
                rows_ref[...].reshape(each, 4, 4, 8, co).astype(jnp.bfloat16)
            )


def body(latents, neighbours, owners, conv_weight, step_embed, up_weight):
    rows_n = lax.axis_size("row")
    cols_n = lax.axis_size("col")
    slots, edge, chan = latents.shape[3], latents.shape[4], latents.shape[-1]
    plane = edge * edge
    own_out = conv_weight.shape[2]
    co = up_weight.shape[-1]
    smem = pl.BlockSpec(memory_space=SMEM)
    piece = pl.pallas_call(
        quarter_kernel,
        out_shape=jax.ShapeDtypeStruct((own_out, SHARE * chan + chan // 2), jnp.bfloat16),
        in_specs=[smem] + whole(1),
        out_specs=pl.BlockSpec(memory_space=VMEM),
        compiler_params=pltpu.CompilerParams(vmem_limit_bytes=4 * MB),
    )(owners, conv_weight.transpose(0, 2, 1))
    lat = latents.reshape(slots, edge, plane, chan)
    def bf16(*shape):
        return jax.ShapeDtypeStruct(shape, jnp.bfloat16)

    fi, faces, give, cross, keep = pl.pallas_call(
        norm_kernel,
        out_shape=[
            bf16(*lat.shape),
            bf16(6, slots, plane, chan),
            bf16(3, slots, plane, chan),
            bf16(slots, plane, chan),
            bf16(2, slots, plane, chan),
        ],
        in_specs=whole(1),
        out_specs=whole(5),
        scratch_shapes=[pltpu.VMEM((chan // 128, edge * plane, 128), jnp.float32)],
        compiler_params=pltpu.CompilerParams(vmem_limit_bytes=6 * MB),
        cost_estimate=pl.CostEstimate(flops=4 * MB, bytes_accessed=2 * MB, transcendentals=MB),
    )(lat)
    swap = [(r, r ^ 1) for r in range(rows_n)]
    between = [(r, r + 1 - 2 * (1 - r % 2)) for r in range(1, rows_n - 1)]
    met = lax.ppermute(give, "row", swap)
    crossed = lax.ppermute(cross, "row", between)
    piece, met = lax.optimization_barrier((piece, met))
    own_w = lax.all_gather(piece, "row", axis=0, tiled=True)
    x_send, z_send = pl.pallas_call(
        pack_kernel,
        out_shape=[bf16(chan, (SHARE + PART) * chan // 2 + 2 * chan)] * 2,
        in_specs=whole(3),
        out_specs=whole(2),
        compiler_params=pltpu.CompilerParams(vmem_limit_bytes=4 * MB),
        cost_estimate=pl.CostEstimate(flops=0, bytes_accessed=4 * MB, transcendentals=0),
    )(own_w, keep, met)
    depth_n = lax.axis_size("depth")
    x_pairs = [
        (d * rows_n + r, (d + 1 - 2 * (r % 2)) % depth_n * rows_n + r)
        for d in range(depth_n)
        for r in range(rows_n)
    ]
    z_pairs = [
        (r * cols_n + c, r * cols_n + (c + 1 - 2 * (r % 2)) % cols_n)
        for r in range(rows_n)
        for c in range(cols_n)
    ]
    x_got = lax.ppermute(x_send, ("depth", "row"), x_pairs)
    z_got = lax.ppermute(z_send, ("row", "col"), z_pairs)
    x_got, crossed = lax.optimization_barrier((x_got, crossed))
    x_other = lax.ppermute(x_got, "row", swap)
    z_other = lax.ppermute(z_got, "row", swap)

    columns = pl.pallas_call(
        columns_kernel,
        out_shape=bf16(19, slots, edge + 2, plane, chan // 2),
        in_specs=[smem] + whole(8),
        out_specs=pl.BlockSpec(memory_space=VMEM),
        scratch_shapes=[
            pltpu.VMEM((6, 2 * slots + 1, plane, chan), jnp.bfloat16),
            pltpu.VMEM((2, plane, chan), jnp.float32),
            pltpu.VMEM((2, plane, chan), jnp.float32),
        ],
        compiler_params=pltpu.CompilerParams(vmem_limit_bytes=8 * MB),
        cost_estimate=pl.CostEstimate(flops=16 * MB, bytes_accessed=6 * MB, transcendentals=0),
    )(neighbours, fi, faces, met, crossed, x_got, z_got, x_other, z_other)

    send_cap = 2
    outgoing = pl.pallas_call(
        conv_kernel,
        out_shape=bf16(rows_n * send_cap, plane, chan),
        in_specs=[smem] + whole(8),
        out_specs=pl.BlockSpec(memory_space=pl.ANY),
        scratch_shapes=[
            pltpu.VMEM((rows_n * send_cap + 1, plane, chan), jnp.bfloat16),
            pltpu.SemaphoreType.DMA,
        ],
        compiler_params=pltpu.CompilerParams(vmem_limit_bytes=26 * MB),
        cost_estimate=pl.CostEstimate(flops=5600 * MB, bytes_accessed=8 * MB, transcendentals=0),
    )(owners, columns, own_w, x_got, z_got, x_other, z_other, lat, step_embed.reshape(1, chan))

    arrived = lax.all_to_all(
        outgoing.reshape(rows_n, send_cap * plane, chan), "row", split_axis=0, concat_axis=0, tiled=True
    ).reshape(rows_n * send_cap, plane, chan)

    end = SHARE * chan
    notes = own_w[::own_out, end : end + slots * 8].astype(jnp.int32)
    serial = jnp.arange(slots * 8, dtype=jnp.int32)
    before = serial[None, :] < serial[:, None]
    own_row = lax.axis_index("row")
    mine = (notes >= 0) & (notes // OCAP == own_row)
    again = jnp.any(mine[:, None, :] & before[None], axis=2)
    origin = jnp.arange(rows_n, dtype=jnp.int32)[:, None] * send_cap + again.astype(jnp.int32)
    wanted = jnp.arange(OCAP, dtype=jnp.int32)[:, None, None]
    source = jnp.sum(jnp.where(mine[None] & (notes[None] % OCAP == wanted), origin[None], 0), axis=(1, 2))

    half = edge // 2
    each = 8
    grown = pl.pallas_call(
        grow_kernel,
        grid_spec=pltpu.PrefetchScalarGridSpec(
            num_scalar_prefetch=1,
            grid=(OCAP // each,),
            in_specs=whole(2),
            out_specs=pl.BlockSpec((each, half, 2, half, 2, edge, co), lambda i, s: (i, 0, 0, 0, 0, 0, 0)),
            scratch_shapes=[pltpu.VMEM((each * plane * 2, co), jnp.float32)],
        ),
        out_shape=jax.ShapeDtypeStruct((OCAP, half, 2, half, 2, edge, co), jnp.bfloat16),
        compiler_params=pltpu.CompilerParams(vmem_limit_bytes=12 * MB),
        cost_estimate=pl.CostEstimate(flops=540 * MB, bytes_accessed=4 * MB, transcendentals=0),
    )(source, arrived, up_weight)
    return grown.reshape(1, 1, 1, OCAP, edge, edge, edge, co)


def solution(mesh):
    return jax.shard_map(
        body,
        mesh=mesh,
        in_specs=(
            P("depth", "row", "col", None, None, None, None, None),
            P("depth", "row", "col", None, None),
            P("depth", "row", "col", None, None),
            P(None, None, "row"),
            P(),
            P(),
        ),
        out_specs=P("depth", "row", "col", None, None, None, None, None),
        check_vma=False,
    )
```

```python
import jax
import jax.numpy as jnp
from jax import lax
from jax.experimental import pallas as pl
from jax.experimental.pallas import tpu as pltpu
from jax.sharding import PartitionSpec as P

OCAP = 16
SHARE = 7
PART = 4
VMEM = pltpu.VMEM
SMEM = pltpu.SMEM
MB = 1024 * 1024


def whole(count):
    return [pl.BlockSpec(memory_space=VMEM)] * count


def norm_kernel(lat_ref, fi_ref, faces_ref, give_ref, cross_ref, keep_ref, rows_ref):
    slots, edge, plane, _ = lat_ref.shape
    lanes = rows_ref.shape[-1]
    pieces = rows_ref.shape[0]
    for b in range(slots):
        for z in range(edge):
            v = lat_ref[b, z].astype(jnp.float32)
            mean_square = jnp.mean(v * v, axis=-1, keepdims=True)
            n = v * lax.rsqrt(mean_square + 1e-06)
            s = n / (1.0 + jnp.exp(-n))
            half = s.astype(jnp.bfloat16)
            fi_ref[b, z] = half
            if z == 0:
                faces_ref[1, b] = half
            if z == edge - 1:
                faces_ref[0, b] = half
            for p in range(pieces):
                rows_ref[p, pl.ds(z * plane, plane), :] = s[:, p * lanes : (p + 1) * lanes]
        for p in range(pieces):
            cols = pl.ds(p * lanes, lanes)
            low = rows_ref[p, pl.ds(0, plane, stride=edge), :]
            high = rows_ref[p, pl.ds(edge - 1, plane, stride=edge), :]
            faces_ref[5, b, :, cols] = low.astype(jnp.bfloat16)
            faces_ref[4, b, :, cols] = high.astype(jnp.bfloat16)
            low = [rows_ref[p, pl.ds(z * plane, edge), :] for z in range(edge)]
            faces_ref[3, b, :, cols] = jnp.concatenate(low, axis=0).astype(jnp.bfloat16)
            high = [rows_ref[p, pl.ds(z * plane + plane - edge, edge), :] for z in range(edge)]
            faces_ref[2, b, :, cols] = jnp.concatenate(high, axis=0).astype(jnp.bfloat16)
    core = core_here()
    for kind in range(2):
        keep_ref[kind] = faces_ref[4 * kind + core]
        give_ref[kind] = faces_ref[4 * kind + 1 - core]
    give_ref[2] = faces_ref[2 + core]
    cross_ref[...] = faces_ref[3 - core]


def pack_kernel(own_ref, keep_ref, met_ref, x_ref, z_ref):
    chan = keep_ref.shape[-1]
    lanes = chan // 2
    face = keep_ref.shape[1] * keep_ref.shape[2]
    full, some = SHARE * lanes, PART * lanes
    left = full + some
    for kind, out_ref in ((0, x_ref), (1, z_ref)):
        start = (1 - kind) * full + core_here() * (full - some)
        rest = out_ref.shape[0] - face
        out_ref[:, :full] = own_ref[:, kind * full : (kind + 1) * full]
        out_ref[:, full:left] = own_ref[:, pl.ds(pl.multiple_of(start, lanes), some)]
        out_ref[:face, left : left + chan] = keep_ref[kind].reshape(face, chan)
        out_ref[:face, left + chan :] = met_ref[kind].reshape(face, chan)
        out_ref[face:, left:] = jnp.zeros((rest, 2 * chan), jnp.bfloat16)


def quarter_kernel(owners_ref, weight_ref, out_ref):
    taps, rows, chan = weight_ref.shape
    lanes = chan // 2
    children = owners_ref.shape[-1]
    lane = lax.broadcasted_iota(jnp.int32, (rows, lanes), 1)
    note = jnp.zeros((rows, lanes), jnp.int32)
    for i in range(owners_ref.shape[-2] * children):
        note = jnp.where(lane == i, owners_ref[0, 0, 0, i // children, i % children], note)
    out_ref[:, 2 * SHARE * lanes :] = note.astype(jnp.float32).astype(jnp.bfloat16)
    for half in range(2):
        first = half * 4 * SHARE + colours()[half] * SHARE
        for j in range(SHARE):
            unit = first + j
            taken = weight_ref[jnp.minimum(lax.div(unit, 2), taps - 1)]
            odd = lax.rem(unit, 2) == 1
            at = (half * SHARE + j) * lanes
            out_ref[:, at : at + lanes] = jnp.where(odd, taken[:, lanes:], taken[:, :lanes])


def columns_kernel(
    near_ref, fi_ref, faces_ref, met_ref, crossed_ref, x_ref, z_ref, xo_ref, zo_ref, out_ref, table_ref, ybuf_ref, xbuf_ref
):
    slots, edge, plane, chan = fi_ref.shape
    core = core_here()

    def ridden(ref, which):
        left = ref.shape[1] - (2 - which) * chan
        return ref[: slots * plane, left : left + chan].reshape(slots, plane, chan)

    far = pl.ds(slots, slots)
    for d in range(6):
        table_ref[d, 0:slots] = faces_ref[d]
        table_ref[d, 2 * slots] = jnp.zeros((plane, chan), jnp.bfloat16)
    table_ref[core, far] = ridden(x_ref, 0)
    table_ref[1 - core, far] = ridden(xo_ref, 1)
    table_ref[2 + core, far] = crossed_ref[...]
    table_ref[3 - core, far] = met_ref[2]
    table_ref[4 + core, far] = ridden(z_ref, 0)
    table_ref[5 - core, far] = ridden(zo_ref, 1)
    out_ref[18] = jnp.zeros(out_ref.shape[1:], jnp.bfloat16)
    at_x = lax.rem(lax.broadcasted_iota(jnp.int32, (plane + 2 * edge, chan), 0), edge)
    rows_n = lax.axis_size("row")
    cols_n = lax.axis_size("col")
    own = (lax.axis_index("depth") * rows_n + lax.axis_index("row")) * cols_n + lax.axis_index("col")
    steps = (-rows_n * cols_n, rows_n * cols_n, -cols_n, cols_n, -1, 1)

    def chosen(b, d):
        named = near_ref[0, 0, 0, b, d]
        here = named - own * slots
        there = named - (own + steps[d]) * slots
        is_here = (named >= 0) & (here >= 0) & (here < slots)
        is_there = (named >= 0) & (there >= 0) & (there < slots)
        index = jnp.where(is_here, here, jnp.where(is_there, slots + there, 2 * slots))
        return table_ref[d, index].astype(jnp.float32)

    def put(b, z, rows, left, right):
        zero = jnp.zeros((edge, chan), jnp.float32)

        def spread(halo):
            mid = jnp.broadcast_to(halo[:, None, :], (edge, edge, chan)).reshape(plane, chan)
            return jnp.concatenate([zero, mid, zero], axis=0)

        count = plane + 2 * edge
        moved = (
            jnp.where(at_x == 0, spread(left), pltpu.roll(rows, 1, 0)),
            rows,
            jnp.where(at_x == edge - 1, spread(right), pltpu.roll(rows, count - 1, 0)),
        )
        for dx in range(3):
            low, high = paired(moved[dx])
            for dy in range(3):
                full = octant_rows(low, high, dy).astype(jnp.bfloat16)
                unit = (dy * 3 + dx) * 2
                out_ref[unit, b, z] = full[:, : chan // 2]
                out_ref[unit + 1, b, z] = full[:, chan // 2 :]

    def brick(b, _):
        zero = jnp.zeros((edge, chan), jnp.float32)
        for side in range(2):
            rows = jnp.concatenate([zero, chosen(b, side), zero], axis=0)
            put(b, side * (edge + 1), rows, zero, zero)
            ybuf_ref[side] = chosen(b, 2 + side)
            xbuf_ref[side] = chosen(b, 4 + side)

        def layer(z, _):
            strip = pl.ds(pl.multiple_of(z * edge, edge), edge)
            rows = jnp.concatenate(
                [ybuf_ref[0, strip, :], fi_ref[b, z].astype(jnp.float32), ybuf_ref[1, strip, :]], axis=0
            )
            put(b, z + 1, rows, xbuf_ref[0, strip, :], xbuf_ref[1, strip, :])
            return 0

        lax.fori_loop(0, edge, layer, 0)
        return 0

    lax.fori_loop(0, slots, brick, 0)


def paired(rows):
    edge = 8
    half = edge // 2
    lines = rows.shape[0] // edge
    in_low = lax.rem(lax.broadcasted_iota(jnp.int32, ((lines - 1) * edge, rows.shape[1]), 0), edge) < half
    turned = pltpu.roll(rows.reshape(lines, edge, -1), half, 1).reshape(rows.shape)
    first, second = slice(0, (lines - 1) * edge), slice(edge, lines * edge)
    low = jnp.where(in_low, rows[first], turned[second])
    high = jnp.where(in_low, turned[first], rows[second])
    return low, high


def octant_rows(low, high, start):
    edge = 8
    half = edge // 2
    out = []
    for ky in range(2):
        for side in (low, high):
            for y in range(0, half, 2):
                at = (ky * half + y + start) * edge
                out.append(side[at : at + edge])
    return jnp.concatenate(out, axis=0)


def colours():
    depth, col = lax.axis_index("depth"), lax.axis_index("col")
    return lax.rem(depth + 2 * col, 4), lax.rem(col + 2 * depth, 4)


def core_here():
    return lax.rem(lax.axis_index("row"), 2)


def unit_rows(cols_ref, b, first, count):
    edge, plane, lanes = cols_ref.shape[2] - 2, cols_ref.shape[3], cols_ref.shape[4]
    out = []
    for j in range(count):
        unit = first + j
        live = unit < 54
        which = jnp.where(live, lax.rem(unit, 18), 18)
        layer = jnp.where(live, lax.div(unit, 18), 0)
        out.append(cols_ref[which, b, pl.ds(layer, edge)].reshape(edge * plane, lanes))
    return out


def conv_kernel(
    owners_ref, cols_ref, own_ref, x_ref, z_ref, xo_ref, zo_ref, lat_ref, emb_ref, out_ref, stash_ref, sem
):
    slots, edge, plane, chan = lat_ref.shape
    lanes = cols_ref.shape[4]
    half = edge // 2
    piece = half * half
    core = core_here()
    full, some, rest = SHARE * lanes, PART * lanes, (SHARE - PART) * lanes
    spans = []
    weights = [own_ref[:, : 2 * full]]
    for kind, colour in enumerate(colours()):
        spans.append((kind * 4 * SHARE + colour * SHARE, SHARE))
    late = pl.ds(pl.multiple_of(full + (1 - core) * (some - rest), lanes), rest)
    for kind, got_ref, other_ref in ((0, x_ref, xo_ref), (1, z_ref, zo_ref)):
        near = kind * 4 * SHARE
        cross = (1 - kind) * 4 * SHARE + lax.rem(colours()[1 - kind] + 2, 4) * SHARE
        colour = colours()[kind]
        spans.append((near + lax.rem(colour + 3 + 2 * core, 4) * SHARE, SHARE))
        spans.append((cross + core * (SHARE - PART), PART))
        spans.append((near + lax.rem(colour + 1 + 2 * core, 4) * SHARE, SHARE))
        spans.append((cross + (1 - core) * PART, SHARE - PART))
        weights += [got_ref[:, : full + some], other_ref[:, :full], other_ref[:, late]]
    weight = jnp.concatenate(weights, axis=1)

    targets = [owners_ref[0, 0, 0, i // 8, i % 8] for i in range(slots * 8)]
    target_rows = [lax.shift_right_arithmetic(t, 4) for t in targets]
    spare = out_ref.shape[0]
    for b in range(slots):
        rows = []
        for first, count in spans:
            rows += unit_rows(cols_ref, b, first, count)
        total = lax.dot_general(
            jnp.concatenate(rows, axis=1), weight, (((1,), (1,)), ((), ())), preferred_element_type=jnp.float32
        )
        total += emb_ref[...]
        places = []
        for k in range(8):
            i = b * 8 + k
            rank = 0
            for j in range(i):
                rank += (target_rows[j] == target_rows[i]).astype(jnp.int32)
            places.append(jnp.where(targets[i] >= 0, target_rows[i] * 2 + rank, spare))
        for z in range(edge):
            low, high = paired(lat_ref[b, z].astype(jnp.float32))
            refined = total[z * plane : (z + 1) * plane] + octant_rows(low, high, 0)
            refined = refined.astype(jnp.bfloat16)
            at = (z % half) * piece
            for side in range(4):
                stash_ref[places[z // half * 4 + side], at : at + piece] = refined[
                    side * piece : (side + 1) * piece
                ]
    copy = pltpu.make_async_copy(stash_ref.at[pl.ds(0, spare)], out_ref, sem)
    copy.start()
    copy.wait()


def grow_kernel(source_ref, child_ref, up_ref, out_ref, rows_ref):
    step = pl.program_id(0)
    each = out_ref.shape[0]
    co = up_ref.shape[-1]
    voxels = child_ref.shape[1]
    lhs = jnp.concatenate([child_ref[source_ref[step * each + j]] for j in range(each)], axis=0)
    for pz in range(2):
        for py in range(2):
            p = pz * 4 + py * 2
            mats = jnp.concatenate([up_ref[p], up_ref[p + 1]], axis=1)
            res = jnp.dot(lhs, mats, preferred_element_type=jnp.float32)
            rows_ref[pl.ds(0, each * voxels, stride=2), :] = res[:, :co]
            rows_ref[pl.ds(1, each * voxels, stride=2), :] = res[:, co:]
            out_ref[:, :, pz, :, py] = (
                rows_ref[...].reshape(each, 4, 4, 8, co).astype(jnp.bfloat16)
            )


def body(latents, neighbours, owners, conv_weight, step_embed, up_weight):
    rows_n = lax.axis_size("row")
    cols_n = lax.axis_size("col")
    slots, edge, chan = latents.shape[3], latents.shape[4], latents.shape[-1]
    plane = edge * edge
    own_out = conv_weight.shape[2]
    co = up_weight.shape[-1]
    smem = pl.BlockSpec(memory_space=SMEM)
    piece = pl.pallas_call(
        quarter_kernel,
        out_shape=jax.ShapeDtypeStruct((own_out, SHARE * chan + chan // 2), jnp.bfloat16),
        in_specs=[smem] + whole(1),
        out_specs=pl.BlockSpec(memory_space=VMEM),
        compiler_params=pltpu.CompilerParams(vmem_limit_bytes=4 * MB),
    )(owners, conv_weight.transpose(0, 2, 1))
    lat = latents.reshape(slots, edge, plane, chan)
    def bf16(*shape):
        return jax.ShapeDtypeStruct(shape, jnp.bfloat16)

    fi, faces, give, cross, keep = pl.pallas_call(
        norm_kernel,
        out_shape=[
            bf16(*lat.shape),
            bf16(6, slots, plane, chan),
            bf16(3, slots, plane, chan),
            bf16(slots, plane, chan),
            bf16(2, slots, plane, chan),
        ],
        in_specs=whole(1),
        out_specs=whole(5),
        scratch_shapes=[pltpu.VMEM((chan // 128, edge * plane, 128), jnp.float32)],
        compiler_params=pltpu.CompilerParams(vmem_limit_bytes=6 * MB),
        cost_estimate=pl.CostEstimate(flops=4 * MB, bytes_accessed=2 * MB, transcendentals=MB),
    )(lat)
    swap = [(r, r ^ 1) for r in range(rows_n)]
    between = [(r, r + 1 - 2 * (1 - r % 2)) for r in range(1, rows_n - 1)]
    met = lax.ppermute(give, "row", swap)
    crossed = lax.ppermute(cross, "row", between)
    piece, give = lax.optimization_barrier((piece, give))
    own_w = lax.all_gather(piece, "row", axis=0, tiled=True)
    x_send, z_send = pl.pallas_call(
        pack_kernel,
        out_shape=[bf16(chan, (SHARE + PART) * chan // 2 + 2 * chan)] * 2,
        in_specs=whole(3),
        out_specs=whole(2),
        compiler_params=pltpu.CompilerParams(vmem_limit_bytes=4 * MB),
        cost_estimate=pl.CostEstimate(flops=0, bytes_accessed=4 * MB, transcendentals=0),
    )(own_w, keep, met)
    depth_n = lax.axis_size("depth")
    x_pairs = [
        (d * rows_n + r, (d + 1 - 2 * (r % 2)) % depth_n * rows_n + r)
        for d in range(depth_n)
        for r in range(rows_n)
    ]
    z_pairs = [
        (r * cols_n + c, r * cols_n + (c + 1 - 2 * (r % 2)) % cols_n)
        for r in range(rows_n)
        for c in range(cols_n)
    ]
    x_got = lax.ppermute(x_send, ("depth", "row"), x_pairs)
    z_got = lax.ppermute(z_send, ("row", "col"), z_pairs)
    x_got, crossed = lax.optimization_barrier((x_got, crossed))
    x_other = lax.ppermute(x_got, "row", swap)
    z_other = lax.ppermute(z_got, "row", swap)

    columns = pl.pallas_call(
        columns_kernel,
        out_shape=bf16(19, slots, edge + 2, plane, chan // 2),
        in_specs=[smem] + whole(8),
        out_specs=pl.BlockSpec(memory_space=VMEM),
        scratch_shapes=[
            pltpu.VMEM((6, 2 * slots + 1, plane, chan), jnp.bfloat16),
            pltpu.VMEM((2, plane, chan), jnp.float32),
            pltpu.VMEM((2, plane, chan), jnp.float32),
        ],
        compiler_params=pltpu.CompilerParams(vmem_limit_bytes=8 * MB),
        cost_estimate=pl.CostEstimate(flops=16 * MB, bytes_accessed=6 * MB, transcendentals=0),
    )(neighbours, fi, faces, met, crossed, x_got, z_got, x_other, z_other)

    send_cap = 2
    outgoing = pl.pallas_call(
        conv_kernel,
        out_shape=bf16(rows_n * send_cap, plane, chan),
        in_specs=[smem] + whole(8),
        out_specs=pl.BlockSpec(memory_space=pl.ANY),
        scratch_shapes=[
            pltpu.VMEM((rows_n * send_cap + 1, plane, chan), jnp.bfloat16),
            pltpu.SemaphoreType.DMA,
        ],
        compiler_params=pltpu.CompilerParams(vmem_limit_bytes=26 * MB),
        cost_estimate=pl.CostEstimate(flops=5600 * MB, bytes_accessed=8 * MB, transcendentals=0),
    )(owners, columns, own_w, x_got, z_got, x_other, z_other, lat, step_embed.reshape(1, chan))

    arrived = lax.all_to_all(
        outgoing.reshape(rows_n, send_cap * plane, chan), "row", split_axis=0, concat_axis=0, tiled=True
    ).reshape(rows_n * send_cap, plane, chan)

    end = SHARE * chan
    notes = own_w[::own_out, end : end + slots * 8].astype(jnp.int32)
    serial = jnp.arange(slots * 8, dtype=jnp.int32)
    before = serial[None, :] < serial[:, None]
    own_row = lax.axis_index("row")
    mine = (notes >= 0) & (notes // OCAP == own_row)
    again = jnp.any(mine[:, None, :] & before[None], axis=2)
    origin = jnp.arange(rows_n, dtype=jnp.int32)[:, None] * send_cap + again.astype(jnp.int32)
    wanted = jnp.arange(OCAP, dtype=jnp.int32)[:, None, None]
    source = jnp.sum(jnp.where(mine[None] & (notes[None] % OCAP == wanted), origin[None], 0), axis=(1, 2))

    half = edge // 2
    each = 8
    grown = pl.pallas_call(
        grow_kernel,
        grid_spec=pltpu.PrefetchScalarGridSpec(
            num_scalar_prefetch=1,
            grid=(OCAP // each,),
            in_specs=whole(2),
            out_specs=pl.BlockSpec((each, half, 2, half, 2, edge, co), lambda i, s: (i, 0, 0, 0, 0, 0, 0)),
            scratch_shapes=[pltpu.VMEM((each * plane * 2, co), jnp.float32)],
        ),
        out_shape=jax.ShapeDtypeStruct((OCAP, half, 2, half, 2, edge, co), jnp.bfloat16),
        compiler_params=pltpu.CompilerParams(vmem_limit_bytes=12 * MB),
        cost_estimate=pl.CostEstimate(flops=540 * MB, bytes_accessed=4 * MB, transcendentals=0),
    )(source, arrived, up_weight)
    return grown.reshape(1, 1, 1, OCAP, edge, edge, edge, co)


def solution(mesh):
    return jax.shard_map(
        body,
        mesh=mesh,
        in_specs=(
            P("depth", "row", "col", None, None, None, None, None),
            P("depth", "row", "col", None, None),
            P("depth", "row", "col", None, None),
            P(None, None, "row"),
            P(),
            P(),
        ),
        out_specs=P("depth", "row", "col", None, None, None, None, None),
        check_vma=False,
    )
```
